32 devices in a mesh: vol: 16 (over z, y, core), strip: 2 (over x).
Axes of the slice: x: 2, y: 2, z: 4, core: 2. Of those that a mesh axis runs over, the one named last changes fastest.
Arguments:
- frames: bfloat16 [32, 1, 128, 1024], P('vol', None, 'strip'), may hold values from 0.5 to 4
- kappa: float32 [32], P('vol'), may hold values from 0.3 to 3
Outputs:
- dff: bfloat16 [32, 1, 64, 2, 1024], P(None, None, 'vol', 'strip')
- slope: bfloat16 [32, 1, 64, 2, 1024], P(None, None, 'vol', 'strip')
The draws below stay inside these ranges and needn't reach their ends.
All inputs are finite; a program needn't handle non-finite values.
Results may differ from the reference program's by a relative error of at most 0.0097.
Values may be sent and summed in bfloat16 or wider, within the bound.
A program may use at most 64 MiB of HBM per device.

```python
import math
import jax
import jax.numpy as jnp
from jax import lax

PLANES = 1
NX = 1024
PASSES = 3
BAND = 16
TIMES = 32
SY = 64
NY = 128
N_STRIP = 2


def level_of(key, shape, shards, low, high):
    def one(dim, blocks):
        draws = jax.random.uniform(jax.random.fold_in(jax.random.fold_in(key, 6), dim), (blocks,), jnp.float32, low / len(shards), high / len(shards))
        return jnp.repeat(jnp.exp(draws), shape[dim] // blocks).reshape((-1,) + (1,) * (len(shape) - dim - 1))

    factor_of = one(*shards[0])
    for cut in shards[1:]:
        factor_of = factor_of * one(*cut)
    return factor_of


def setup_inputs(seed: int = 0) -> dict:
    seeds = jax.random.split(jax.random.key(seed), 3)
    return {
        "frames": jnp.clip(jnp.exp(math.log(4.0) - 2.0794415 * jax.random.uniform(seeds[0], (TIMES, PLANES, NY, NX), jnp.float32) ** level_of(seeds[0], (TIMES, PLANES, NY, NX), ((0, 16), (2, 2)), -0.2, 0.2)), 0.5, 4.0).astype(jnp.bfloat16),
        "kappa": jnp.clip(jnp.exp(math.log(3.0) - 2.3025851 * jax.random.uniform(seeds[1], (TIMES,), jnp.float32) ** level_of(seeds[1], (TIMES,), ((0, 16),), -0.2, 0.2)), 0.3, 3.0),
    }


def flux(diff, kap):
    ratio = diff / kap
    return diff / (1.0 + ratio * ratio)


def advance(extended, kap):
    center = extended[..., 1:-1, :]
    upper = extended[..., :-2, :] - center
    lower = extended[..., 2:, :] - center
    padded = jnp.pad(center, [(0, 0)] * (center.ndim - 1) + [(1, 1)])
    left = padded[..., :-2] - center
    right = padded[..., 2:] - center
    total = flux(upper, kap) + flux(lower, kap) + flux(left, kap) + flux(right, kap)
    return center + 0.2 * total


def smooth_weights(times):
    steps = jnp.arange(times, dtype=jnp.int32)
    gap = jnp.abs(steps[:, None] - steps[None, :])
    raw = jnp.where(gap <= BAND, BAND + 1 - gap, 0).astype(jnp.float32)
    return (raw / jnp.sum(raw, axis=1, keepdims=True)).astype(jnp.bfloat16)


def reference(frames, kappa):
    def one_volume(item):
        volume, kap = item
        field = volume.astype(jnp.float32)
        for step in range(PASSES):
            field = advance(jnp.pad(field, ((0, 0), (1, 1), (0, 0))), kap)
        return field.astype(jnp.bfloat16)

    stored = lax.map(one_volume, (frames, kappa))
    weights = smooth_weights(TIMES)

    def one_plane(plane):
        flat = plane.reshape(TIMES, NY * NX)
        baseline = jnp.dot(weights, flat, preferred_element_type=jnp.float32)
        ratio = (flat.astype(jnp.float32) - baseline) / (baseline + 0.1)
        slope = jnp.concatenate([ratio[1:2] - ratio[0:1], (ratio[2:] - ratio[:-2]) * 0.5, ratio[-1:] - ratio[-2:-1]], axis=0)
        return ratio.reshape(TIMES, NY, NX).astype(jnp.bfloat16), slope.reshape(TIMES, NY, NX).astype(jnp.bfloat16)

    ratio, slope = lax.map(one_plane, jnp.transpose(stored, (1, 0, 2, 3)))

    def layout(field):
        field = jnp.transpose(field, (1, 0, 2, 3)).reshape(TIMES, PLANES, N_STRIP, SY, NX)
        return jnp.transpose(field, (0, 1, 3, 2, 4))

    return layout(ratio), layout(slope)
```

```python
import functools

import jax
import jax.numpy as jnp
from jax import lax
from jax.experimental import pallas as pl
from jax.experimental.pallas import tpu as pltpu
from jax.sharding import PartitionSpec as P

PASSES = 3
BAND = 16
LANES = 128
TILE = 8
PACK = 16
MESH = pl.DeviceIdType.MESH


def inverse(value):
    guess = pltpu.reciprocal(value, approx=True)
    return guess * (2.0 - value * guess)


def flux(diff):
    return diff * inverse(1.0 + diff * diff)


def shifted_rows(center, below):
    row = lax.broadcasted_iota(jnp.int32, center.shape, 0)
    return pltpu.roll(jnp.where(row == 0, below, center), TILE - 1, 0)


def flux_x(center):
    nx = center.shape[1]
    lane = lax.broadcasted_iota(jnp.int32, (TILE, LANES), 1)
    left = pltpu.roll(center, 1, 1)
    left = jnp.concatenate([jnp.where(lane == 0, 0.0, left[:, :LANES]), left[:, LANES:]], axis=1)
    into = flux(left - center)
    out = pltpu.roll(into, nx - 1, 1)
    edge = flux(center[:, nx - LANES :])
    out = jnp.concatenate([out[:, : nx - LANES], jnp.where(lane == LANES - 1, edge, out[:, nx - LANES :])], axis=1)
    return into - out


def advance(field, tiles, emit):
    row = lax.broadcasted_iota(jnp.int32, (TILE, field.shape[-1]), 0)

    def tile(i):
        i = i % (tiles + 1)
        return field[i * TILE : (i + 1) * TILE, :]

    first = tile(0)
    last = tile(tiles)
    before = flux(shifted_rows(last, first) - last)
    for i in range(tiles + 1):
        center = tile(i)
        down = flux(shifted_rows(center, tile(i + 1)) - center)
        up = pltpu.roll(jnp.where(row == TILE - 1, before, down), 1, 0)
        total = (down - up) + flux_x(center)
        emit(i, center + 0.2 * total)
        before = down


def kernel(n, strips, frames, kappa, dff, slope, held, kap, halo, field, send, recv, mix, ratio,
           load_sem, halo_send, halo_recv, send_sem, recv_sem, own_sem):
    vols, _, rows, nx = frames.shape
    times = recv.shape[0]
    tiles = rows // TILE
    me = lax.axis_index("vol")
    strip = lax.axis_index("strip")
    has_up = strip > 0
    has_down = strip < strips - 1

    load = pltpu.make_async_copy(frames.at[:, 0], held, load_sem.at[0])
    load_kappa = pltpu.make_async_copy(kappa, kap, load_sem.at[1])
    load.start()
    load_kappa.start()

    barrier = pltpu.get_barrier_semaphore()

    @pl.loop(1, n)
    def _(k):
        pl.semaphore_signal(barrier, inc=1, device_id={"vol": lax.rem(me + k, n)}, device_id_type=MESH)

    @pl.when(has_up)
    def _():
        pl.semaphore_signal(barrier, inc=1, device_id={"strip": strip - 1}, device_id_type=MESH)

    @pl.when(has_down)
    def _():
        pl.semaphore_signal(barrier, inc=1, device_id={"strip": strip + 1}, device_id_type=MESH)

    load.wait()
    load_kappa.wait()

    for v in range(vols):
        scale = 1.0 / jnp.full((PACK, nx), kap[v], jnp.float32)
        for i in range(rows // PACK):
            part = pl.ds(i * PACK, PACK)
            field[0, v, part, :] = held[v, part, :].astype(jnp.float32) * scale

    pl.semaphore_wait(barrier, n - 1 + has_up.astype(jnp.int32) + has_down.astype(jnp.int32))

    def to_up():
        return pltpu.make_async_remote_copy(
            src_ref=held.at[:, pl.ds(0, PACK)], dst_ref=halo.at[1],
            send_sem=halo_send.at[1], recv_sem=halo_recv.at[1],
            device_id={"strip": strip - 1}, device_id_type=MESH)

    def to_down():
        return pltpu.make_async_remote_copy(
            src_ref=held.at[:, pl.ds(rows - PACK, PACK)], dst_ref=halo.at[0],
            send_sem=halo_send.at[0], recv_sem=halo_recv.at[0],
            device_id={"strip": strip + 1}, device_id_type=MESH)

    @pl.when(has_up)
    def _():
        to_up().start()

    @pl.when(has_down)
    def _():
        to_down().start()

    column = lax.broadcasted_iota(jnp.int32, (PACK, times * PACK), 1)
    diagonal = column % PACK == lax.broadcasted_iota(jnp.int32, (PACK, times * PACK), 0)
    source = column // PACK

    @pl.loop(0, times)
    def _(t):
        ahead = jnp.maximum(BAND - t, 0)
        behind = jnp.maximum(t + BAND + 1 - times, 0)
        total = (BAND + 1) ** 2 - (ahead * (ahead + 1) + behind * (behind + 1)) // 2
        raw = jnp.maximum(BAND + 1 - jnp.abs(source - t), 0).astype(jnp.float32)
        weight = raw / jnp.full(raw.shape, total, jnp.int32).astype(jnp.float32)
        mix[pl.ds(pl.multiple_of(t * PACK, PACK), PACK), :] = jnp.where(diagonal, weight, 0.0).astype(jnp.bfloat16)

    edge = lax.broadcasted_iota(jnp.int32, (TILE, nx), 0)
    ring = pl.ds(rows, TILE)
    for v in range(vols):
        field[0, v, ring, :] = jnp.zeros((TILE, nx), jnp.float32)

    @pl.when(has_up)
    def _():
        to_down().wait_recv()
        for v in range(vols):
            scale = 1.0 / jnp.full((TILE, nx), kap[v], jnp.float32)
            value = halo[0, v].astype(jnp.float32)[PACK - TILE :] * scale
            field[0, v, ring, :] = jnp.where(edge >= TILE - PASSES, value, 0.0)

    @pl.when(has_down)
    def _():
        to_up().wait_recv()
        for v in range(vols):
            scale = 1.0 / jnp.full((TILE, nx), kap[v], jnp.float32)
            value = halo[1, v].astype(jnp.float32)[:TILE] * scale
            field[0, v, ring, :] = jnp.where(edge < PASSES, value, field[0, v, ring, :])

    inside = jnp.where(edge < TILE // 2, jnp.full(edge.shape, has_down.astype(jnp.int32)),
                       jnp.full(edge.shape, has_up.astype(jnp.int32))) > 0
    small = lax.broadcasted_iota(jnp.int32, (TILE, LANES), 0) < TILE // 2
    chunks = nx // LANES

    @pl.loop(0, vols)
    def _(v):
        for step in range(PASSES - 1):
            target = field.at[(step + 1) % 2, v]

            def keep(i, value):
                if i == tiles:
                    value = jnp.where(inside, value, 0.0)
                target[i * TILE : (i + 1) * TILE, :] = value

            advance(field.at[step % 2, v], tiles, keep)

        unscale = jnp.full((TILE, nx), kap[v], jnp.float32)

        def pack(i, value):
            if i == tiles:
                return
            value = value * unscale
            swapped = pltpu.roll(value, TILE // 2, 0)
            upper, lower = [], []
            for c in range(0, chunks, 2):
                a, b = slice(c * LANES, (c + 1) * LANES), slice((c + 1) * LANES, (c + 2) * LANES)
                upper.append(jnp.where(small, value[:, a], swapped[:, b]))
                lower.append(jnp.where(small, swapped[:, a], value[:, b]))
            send[v, 2 * i] = jnp.concatenate(upper, axis=0).astype(jnp.bfloat16)
            send[v, 2 * i + 1] = jnp.concatenate(lower, axis=0).astype(jnp.bfloat16)

        advance(field.at[(PASSES - 1) % 2, v], tiles, pack)

        @pl.loop(1, n)
        def _(k):
            to = lax.rem(me + k, n)
            pltpu.make_async_remote_copy(
                src_ref=send.at[v, to], dst_ref=recv.at[me * vols + v],
                send_sem=send_sem.at[v], recv_sem=recv_sem.at[v],
                device_id={"vol": to}, device_id_type=MESH).start()

        pltpu.make_async_copy(send.at[v, me], recv.at[me * vols + v], own_sem.at[v]).start()

    def all_of(v):
        return pltpu.make_async_remote_copy(
            src_ref=send.at[v, pl.ds(0, n - 1)], dst_ref=recv.at[pl.ds(0, n - 1)],
            send_sem=send_sem.at[v], recv_sem=recv_sem.at[v],
            device_id={"vol": lax.rem(me + 1, n)}, device_id_type=MESH)

    for v in range(vols):
        pltpu.make_async_copy(send.at[v, me], recv.at[me * vols + v], own_sem.at[v]).wait()
        all_of(v).wait_recv()

    halves = recv.shape[1] // PACK
    values = jnp.concatenate(
        [recv[:, h * PACK : (h + 1) * PACK, :].reshape(times * PACK, LANES) for h in range(halves)], axis=1)
    block = min(times, 32)
    for start in range(0, times, block):
        these = pl.ds(start, block)
        base = jnp.dot(mix[start * PACK : (start + block) * PACK, :], values, preferred_element_type=jnp.float32)
        for h in range(halves):
            part = base[:, h * LANES : (h + 1) * LANES].reshape(block, PACK, LANES)
            span = slice(h * PACK, (h + 1) * PACK)
            stored = recv[these, span, :].astype(jnp.float32)
            got = (stored - part) * inverse(part + 0.1)
            ratio[these, span, :] = got
            dff[these, span, :] = got.astype(jnp.bfloat16)

    slope[0] = (ratio[1] - ratio[0]).astype(jnp.bfloat16)
    slope[1 : times - 1] = ((ratio[2:] - ratio[: times - 2]) * 0.5).astype(jnp.bfloat16)
    slope[times - 1] = (ratio[times - 1] - ratio[times - 2]).astype(jnp.bfloat16)

    for v in range(vols):
        all_of(v).wait_send()

    @pl.when(has_up)
    def _():
        to_up().wait_send()

    @pl.when(has_down)
    def _():
        to_down().wait_send()


def local(n, strips, frames, kappa):
    vols, planes, rows, nx = frames.shape
    times = vols * n
    each = rows // n
    assert planes == 1 and each * 2 == TILE and nx % (2 * LANES) == 0
    depth = each * nx // LANES
    out = jax.ShapeDtypeStruct((times, depth, LANES), jnp.bfloat16)
    f32, bf16 = jnp.float32, jnp.bfloat16
    results = pl.pallas_call(
        functools.partial(kernel, n, strips),
        out_shape=(out, out),
        in_specs=[pl.BlockSpec(memory_space=pl.ANY)] * 2,
        out_specs=(pl.BlockSpec(memory_space=pltpu.VMEM),) * 2,
        scratch_shapes=[
            pltpu.VMEM((vols, rows, nx), bf16),
            pltpu.SMEM((vols,), f32),
            pltpu.VMEM((2, vols, PACK, nx), bf16),
            pltpu.VMEM((2, vols, rows + TILE, nx), f32),
            pltpu.VMEM((vols, n, depth, LANES), bf16),
            pltpu.VMEM((times, depth, LANES), bf16),
            pltpu.VMEM((times * PACK, times * PACK), bf16),
            pltpu.VMEM((times, depth, LANES), f32),
            pltpu.SemaphoreType.DMA((2,)),
            pltpu.SemaphoreType.DMA((2,)),
            pltpu.SemaphoreType.DMA((2,)),
            pltpu.SemaphoreType.DMA((vols,)),
            pltpu.SemaphoreType.DMA((vols,)),
            pltpu.SemaphoreType.DMA((vols,)),
        ],
        compiler_params=pltpu.CompilerParams(
            collective_id=0, has_side_effects=True, vmem_limit_bytes=48 * 1024 * 1024),
        cost_estimate=pl.CostEstimate(flops=200_000_000, bytes_accessed=1_000_000, transcendentals=1_000_000),
    )(frames, kappa)

    def laid(value):
        value = value.reshape(times, nx // LANES, each, LANES).transpose(0, 2, 1, 3)
        return value.reshape(times, 1, each, 1, nx)

    return laid(results[0]), laid(results[1])


def solution(mesh):
    placed = P(None, None, "vol", "strip", None)
    return jax.shard_map(
        functools.partial(local, mesh.shape["vol"], mesh.shape["strip"]),
        mesh=mesh,
        in_specs=(P("vol", None, "strip", None), P("vol")),
        out_specs=(placed, placed),
        check_vma=False,
    )
```

```python
import functools

import jax
import jax.numpy as jnp
from jax import lax
from jax.experimental import pallas as pl
from jax.experimental.pallas import tpu as pltpu
from jax.sharding import PartitionSpec as P

PASSES = 3
BAND = 16
LANES = 128
TILE = 8
PACK = 16
MESH = pl.DeviceIdType.MESH


def inverse(value):
    guess = pltpu.reciprocal(value, approx=True)
    return guess * (2.0 - value * guess)


def flux(diff):
    return diff * inverse(1.0 + diff * diff)


def shifted_rows(center, below):
    row = lax.broadcasted_iota(jnp.int32, center.shape, 0)
    return pltpu.roll(jnp.where(row == 0, below, center), TILE - 1, 0)


def flux_x(center):
    nx = center.shape[1]
    lane = lax.broadcasted_iota(jnp.int32, (TILE, LANES), 1)
    left = pltpu.roll(center, 1, 1)
    left = jnp.concatenate([jnp.where(lane == 0, 0.0, left[:, :LANES]), left[:, LANES:]], axis=1)
    into = flux(left - center)
    out = pltpu.roll(into, nx - 1, 1)
    edge = flux(center[:, nx - LANES :])
    out = jnp.concatenate([out[:, : nx - LANES], jnp.where(lane == LANES - 1, edge, out[:, nx - LANES :])], axis=1)
    return into - out


def advance(tiles, emit):
    count = len(tiles)
    center = tiles[0]()
    zero = jnp.zeros_like(center)
    row = lax.broadcasted_iota(jnp.int32, center.shape, 0)
    before = flux(shifted_rows(zero, center))
    for i in range(count):
        below = tiles[i + 1]() if i + 1 < count else zero
        down = flux(shifted_rows(center, below) - center)
        up = pltpu.roll(jnp.where(row == TILE - 1, before, down), 1, 0)
        total = (down - up) + flux_x(center)
        emit(i, center + 0.2 * total)
        before, center = down, below


def folded(value, lower):
    small = lax.broadcasted_iota(jnp.int32, (TILE, LANES), 0) < TILE // 2
    swapped = pltpu.roll(value, TILE // 2, 0)
    first, second = (swapped, value) if lower else (value, swapped)
    parts = []
    for c in range(0, value.shape[1], 2 * LANES):
        parts.append(jnp.where(small, first[:, c : c + LANES], second[:, c + LANES : c + 2 * LANES]))
    return jnp.concatenate(parts, axis=0).astype(jnp.bfloat16)


def kernel(n, strips, frames, kappa, dff, slope, held, kap, halo, field, send, recv, mix, ratio,
           load_sem, halo_send, halo_recv, send_sem, recv_sem, own_sem):
    vols, _, rows, nx = frames.shape
    times, depth, _ = recv.shape
    tiles = rows // TILE
    me = lax.axis_index("vol")
    strip = lax.axis_index("strip")
    has_up = strip > 0
    has_down = strip < strips - 1

    loads = [pltpu.make_async_copy(frames.at[v, 0], held.at[v], load_sem.at[v]) for v in range(vols)]
    load_kappa = pltpu.make_async_copy(kappa, kap, load_sem.at[vols])
    load_kappa.start()
    for load in loads:
        load.start()

    barrier = pltpu.get_barrier_semaphore()

    @pl.loop(1, n)
    def _(k):
        pl.semaphore_signal(barrier, inc=1, device_id={"vol": lax.rem(me + k, n)}, device_id_type=MESH)

    @pl.when(has_up)
    def _():
        pl.semaphore_signal(barrier, inc=1, device_id={"strip": strip - 1}, device_id_type=MESH)

    @pl.when(has_down)
    def _():
        pl.semaphore_signal(barrier, inc=1, device_id={"strip": strip + 1}, device_id_type=MESH)

    def to_up():
        return pltpu.make_async_remote_copy(
            src_ref=frames.at[:, 0, pl.ds(0, PACK)], dst_ref=halo.at[1],
            send_sem=halo_send.at[1], recv_sem=halo_recv.at[1],
            device_id={"strip": strip - 1}, device_id_type=MESH)

    def to_down():
        return pltpu.make_async_remote_copy(
            src_ref=frames.at[:, 0, pl.ds(rows - PACK, PACK)], dst_ref=halo.at[0],
            send_sem=halo_send.at[0], recv_sem=halo_recv.at[0],
            device_id={"strip": strip + 1}, device_id_type=MESH)

    parts = depth // PACK
    pieces = [(v, 0, depth) for v in range(vols - 1)] + [(vols - 1, p * PACK, PACK) for p in range(parts)]

    def sending(piece, to):
        v, start, length = pieces[piece]
        return pltpu.make_async_remote_copy(
            src_ref=send.at[v, to, pl.ds(start, length)], dst_ref=recv.at[me * vols + v, pl.ds(start, length)],
            send_sem=send_sem.at[piece], recv_sem=recv_sem.at[piece],
            device_id={"vol": to}, device_id_type=MESH)

    def all_of(piece):
        _, start, length = pieces[piece]
        return pltpu.make_async_remote_copy(
            src_ref=send.at[0, pl.ds(0, n - 1), pl.ds(start, length)], dst_ref=recv.at[pl.ds(0, n - 1), pl.ds(start, length)],
            send_sem=send_sem.at[piece], recv_sem=recv_sem.at[piece],
            device_id={"vol": lax.rem(me + 1, n)}, device_id_type=MESH)

    def scaled(block, v):
        return block.astype(jnp.float32) * (1.0 / jnp.full(block.shape, kap[v], jnp.float32))

    def getters(v, step):
        if step == 0:
            cache = {}

            def get(i):
                if i // 2 not in cache:
                    cache[i // 2] = scaled(held[v, (i // 2) * PACK : (i // 2 + 1) * PACK, :], v)
                return cache[i // 2][i % 2 * TILE : i % 2 * TILE + TILE]
        else:
            def get(i):
                return field[(step - 1) % 2, v, i * TILE : (i + 1) * TILE, :]
        return [functools.partial(get, i) for i in range(tiles)]

    load_kappa.wait()
    for v in range(vols):
        loads[v].wait()
        unscale = jnp.full((TILE, nx), kap[v], jnp.float32)
        for step in range(PASSES):
            def emit(i, value, v=v, step=step):
                if step < PASSES - 1:
                    field[step % 2, v, i * TILE : (i + 1) * TILE, :] = value
                else:
                    value = value * unscale
                    send[v, 2 * i] = folded(value, False)
                    send[v, 2 * i + 1] = folded(value, True)

            advance(getters(v, step), emit)

        if v == 0:
            pl.semaphore_wait(barrier, n - 1 + has_up.astype(jnp.int32) + has_down.astype(jnp.int32))

            @pl.when(has_up)
            def _():
                to_up().start()

            @pl.when(has_down)
            def _():
                to_down().start()

        for piece, (volume, _, _) in enumerate(pieces):
            if volume != v:
                continue

            @pl.loop(0, n - 1)
            def _(j):
                away = (j + 1) // 2
                to = lax.rem(me + n // 2 + n + jnp.where(j % 2 == 1, away, -away), n)

                @pl.when(jnp.logical_and(to > 0, to < n - 1))
                def _():
                    sending(piece, to).start()

    def edge(own, other, own_first, v):
        both = [own, other] if own_first else [other, own]
        for step in range(PASSES):
            made = []
            advance([lambda x=x: x for x in both], lambda i, value: made.append(value))
            both = made
        return both[0 if own_first else 1] * jnp.full(own.shape, kap[v], jnp.float32)

    @pl.when(has_up)
    def _():
        to_down().wait_recv()
        for v in range(vols):
            beyond = scaled(halo[0, v], v)[PACK - TILE :]
            mine = scaled(held[v, :PACK, :], v)[:TILE]
            send[v, 0] = folded(edge(mine, beyond, False, v), False)

    @pl.when(has_down)
    def _():
        to_up().wait_recv()
        for v in range(vols):
            beyond = scaled(halo[1, v], v)[:TILE]
            mine = scaled(held[v, rows - PACK : rows, :], v)[PACK - TILE :]
            send[v, n - 1] = folded(edge(mine, beyond, True, v), True)

    for to in (0, n - 1):
        @pl.when(me != to)
        def _():
            for piece in range(len(pieces)):
                sending(piece, to).start()

    own = [pltpu.make_async_copy(send.at[v, me], recv.at[me * vols + v], own_sem.at[v]) for v in range(vols)]
    for copy in own:
        copy.start()

    column = lax.broadcasted_iota(jnp.int32, (PACK, times * PACK), 1)
    diagonal = column % PACK == lax.broadcasted_iota(jnp.int32, (PACK, times * PACK), 0)
    source = column // PACK

    @pl.loop(0, times)
    def _(t):
        ahead = jnp.maximum(BAND - t, 0)
        behind = jnp.maximum(t + BAND + 1 - times, 0)
        total = (BAND + 1) ** 2 - (ahead * (ahead + 1) + behind * (behind + 1)) // 2
        raw = jnp.maximum(BAND + 1 - jnp.abs(source - t), 0).astype(jnp.float32)
        weight = raw / jnp.full(raw.shape, total, jnp.int32).astype(jnp.float32)
        mix[pl.ds(pl.multiple_of(t * PACK, PACK), PACK), :] = jnp.where(diagonal, weight, 0.0).astype(jnp.bfloat16)

    for copy in own:
        copy.wait()
    for piece in range(vols - 1):
        all_of(piece).wait_recv()

    block = min(times, 32)
    for p in range(parts):
        all_of(vols - 1 + p).wait_recv()
        span = slice(p * PACK, (p + 1) * PACK)
        values = recv[:, span, :].reshape(times * PACK, LANES)
        for start in range(0, times, block):
            these = pl.ds(start, block)
            base = jnp.dot(mix[start * PACK : (start + block) * PACK, :], values, preferred_element_type=jnp.float32)
            base = base.reshape(block, PACK, LANES)
            got = (recv[these, span, :].astype(jnp.float32) - base) * inverse(base + 0.1)
            ratio[these, span, :] = got
            dff[these, span, :] = got.astype(jnp.bfloat16)
        slope[0, span] = (ratio[1, span] - ratio[0, span]).astype(jnp.bfloat16)
        slope[1 : times - 1, span] = ((ratio[2:, span] - ratio[: times - 2, span]) * 0.5).astype(jnp.bfloat16)
        slope[times - 1, span] = (ratio[times - 1, span] - ratio[times - 2, span]).astype(jnp.bfloat16)

    for piece in range(len(pieces)):
        all_of(piece).wait_send()

    @pl.when(has_up)
    def _():
        to_up().wait_send()

    @pl.when(has_down)
    def _():
        to_down().wait_send()


def local(n, strips, frames, kappa):
    vols, planes, rows, nx = frames.shape
    times = vols * n
    each = rows // n
    assert planes == 1 and each * 2 == TILE and nx % (2 * LANES) == 0
    depth = each * nx // LANES
    pieces = vols - 1 + depth // PACK
    out = jax.ShapeDtypeStruct((times, depth, LANES), jnp.bfloat16)
    f32, bf16 = jnp.float32, jnp.bfloat16
    results = pl.pallas_call(
        functools.partial(kernel, n, strips),
        out_shape=(out, out),
        in_specs=[pl.BlockSpec(memory_space=pltpu.HBM)] * 2,
        out_specs=(pl.BlockSpec(memory_space=pltpu.VMEM),) * 2,
        scratch_shapes=[
            pltpu.VMEM((vols, rows, nx), bf16),
            pltpu.SMEM((vols,), f32),
            pltpu.VMEM((2, vols, PACK, nx), bf16),
            pltpu.VMEM((2, vols, rows, nx), f32),
            pltpu.VMEM((vols, n, depth, LANES), bf16),
            pltpu.VMEM((times, depth, LANES), bf16),
            pltpu.VMEM((times * PACK, times * PACK), bf16),
            pltpu.VMEM((times, depth, LANES), f32),
            pltpu.SemaphoreType.DMA((vols + 1,)),
            pltpu.SemaphoreType.DMA((2,)),
            pltpu.SemaphoreType.DMA((2,)),
            pltpu.SemaphoreType.DMA((pieces,)),
            pltpu.SemaphoreType.DMA((pieces,)),
            pltpu.SemaphoreType.DMA((vols,)),
        ],
        compiler_params=pltpu.CompilerParams(
            collective_id=0, has_side_effects=True, vmem_limit_bytes=62 * 1024 * 1024),
        cost_estimate=pl.CostEstimate(flops=200_000_000, bytes_accessed=1_000_000, transcendentals=1_000_000),
    )(frames, kappa)

    def laid(value):
        value = value.reshape(times, nx // LANES, each, LANES).transpose(0, 2, 1, 3)
        return value.reshape(times, 1, each, 1, nx)

    return laid(results[0]), laid(results[1])


def solution(mesh):
    placed = P(None, None, "vol", "strip", None)
    return jax.shard_map(
        functools.partial(local, mesh.shape["vol"], mesh.shape["strip"]),
        mesh=mesh,
        in_specs=(P("vol", None, "strip", None), P("vol")),
        out_specs=(placed, placed),
        check_vma=False,
    )
```

```python
import functools

import jax
import jax.numpy as jnp
from jax import lax
from jax.experimental import pallas as pl
from jax.experimental.pallas import tpu as pltpu
from jax.sharding import PartitionSpec as P

PASSES = 3
BAND = 16
LANES = 128
TILE = 8
PACK = 16
MESH = pl.DeviceIdType.MESH


def inverse(value):
    guess = pltpu.reciprocal(value, approx=True)
    return guess * (2.0 - value * guess)


def flux(diff):
    return diff * inverse(1.0 + diff * diff)


def shifted_rows(center, below):
    row = lax.broadcasted_iota(jnp.int32, center.shape, 0)
    return pltpu.roll(jnp.where(row == 0, below, center), TILE - 1, 0)


def flux_x(center):
    nx = center.shape[1]
    lane = lax.broadcasted_iota(jnp.int32, (TILE, LANES), 1)
    left = pltpu.roll(center, 1, 1)
    left = jnp.concatenate([jnp.where(lane == 0, 0.0, left[:, :LANES]), left[:, LANES:]], axis=1)
    into = flux(left - center)
    out = pltpu.roll(into, nx - 1, 1)
    edge = flux(center[:, nx - LANES :])
    out = jnp.concatenate([out[:, : nx - LANES], jnp.where(lane == LANES - 1, edge, out[:, nx - LANES :])], axis=1)
    return into - out


def advance(tiles, emit):
    count = len(tiles)
    center = tiles[0]()
    zero = jnp.zeros_like(center)
    row = lax.broadcasted_iota(jnp.int32, center.shape, 0)
    before = flux(shifted_rows(zero, center))
    for i in range(count):
        below = tiles[i + 1]() if i + 1 < count else zero
        down = flux(shifted_rows(center, below) - center)
        up = pltpu.roll(jnp.where(row == TILE - 1, before, down), 1, 0)
        total = (down - up) + flux_x(center)
        emit(i, center + 0.2 * total)
        before, center = down, below


def folded(value, lower):
    small = lax.broadcasted_iota(jnp.int32, (TILE, LANES), 0) < TILE // 2
    swapped = pltpu.roll(value, TILE // 2, 0)
    first, second = (swapped, value) if lower else (value, swapped)
    parts = []
    for c in range(0, value.shape[1], 2 * LANES):
        parts.append(jnp.where(small, first[:, c : c + LANES], second[:, c + LANES : c + 2 * LANES]))
    return jnp.concatenate(parts, axis=0).astype(jnp.bfloat16)


def kernel(n, strips, frames, kappa, dff, slope, held, kap, halo, field, send, recv, mix, ratio,
           load_sem, halo_send, halo_recv, send_sem, recv_sem, own_sem):
    vols, _, rows, nx = frames.shape
    times, depth, _ = recv.shape
    tiles = rows // TILE
    me = lax.axis_index("vol")
    strip = lax.axis_index("strip")
    has_up = strip > 0
    has_down = strip < strips - 1

    loads = [pltpu.make_async_copy(frames.at[v, 0], held.at[v], load_sem.at[v]) for v in range(vols)]
    load_kappa = pltpu.make_async_copy(kappa, kap, load_sem.at[vols])
    load_kappa.start()
    for load in loads:
        load.start()

    barrier = pltpu.get_barrier_semaphore()

    @pl.loop(1, n)
    def _(k):
        pl.semaphore_signal(barrier, inc=1, device_id={"vol": lax.rem(me + k, n)}, device_id_type=MESH)

    @pl.when(has_up)
    def _():
        pl.semaphore_signal(barrier, inc=1, device_id={"strip": strip - 1}, device_id_type=MESH)

    @pl.when(has_down)
    def _():
        pl.semaphore_signal(barrier, inc=1, device_id={"strip": strip + 1}, device_id_type=MESH)

    def to_up():
        return pltpu.make_async_remote_copy(
            src_ref=frames.at[:, 0, pl.ds(0, PACK)], dst_ref=halo.at[1],
            send_sem=halo_send.at[1], recv_sem=halo_recv.at[1],
            device_id={"strip": strip - 1}, device_id_type=MESH)

    def to_down():
        return pltpu.make_async_remote_copy(
            src_ref=frames.at[:, 0, pl.ds(rows - PACK, PACK)], dst_ref=halo.at[0],
            send_sem=halo_send.at[0], recv_sem=halo_recv.at[0],
            device_id={"strip": strip + 1}, device_id_type=MESH)

    parts = depth // PACK
    pieces = [(v, 0, depth) for v in range(vols - 1)] + [(vols - 1, p * PACK, PACK) for p in range(parts)]

    def sending(v, start, length, piece, to):
        return pltpu.make_async_remote_copy(
            src_ref=send.at[v, to, pl.ds(start, length)], dst_ref=recv.at[me * vols + v, pl.ds(start, length)],
            send_sem=send_sem.at[piece], recv_sem=recv_sem.at[piece],
            device_id={"vol": to}, device_id_type=MESH)

    def all_of(piece):
        _, start, length = pieces[piece]
        return pltpu.make_async_remote_copy(
            src_ref=send.at[0, pl.ds(0, n - 1), pl.ds(start, length)], dst_ref=recv.at[pl.ds(0, n - 1), pl.ds(start, length)],
            send_sem=send_sem.at[piece], recv_sem=recv_sem.at[piece],
            device_id={"vol": lax.rem(me + 1, n)}, device_id_type=MESH)

    def scaled(block, v):
        return block.astype(jnp.float32) * (1.0 / jnp.full(block.shape, kap[v], jnp.float32))

    def getters(v, step):
        if step == 0:
            cache = {}

            def get(i):
                if i // 2 not in cache:
                    cache[i // 2] = scaled(held[v, (i // 2) * PACK : (i // 2 + 1) * PACK, :], v)
                return cache[i // 2][i % 2 * TILE : i % 2 * TILE + TILE]
        else:
            def get(i):
                return field[(step - 1) % 2, i * TILE : (i + 1) * TILE, :]
        return [functools.partial(get, i) for i in range(tiles)]

    def order(body):
        def step(j, _):
            away = (j + 1) // 2
            body(lax.rem(me + n // 2 + n + jnp.where(j % 2 == 1, away, -away), n))
            return _

        lax.fori_loop(0, n - 1, step, 0, unroll=n <= 16)

    load_kappa.wait()

    @pl.loop(0, vols)
    def _(v):
        pltpu.make_async_copy(frames.at[v, 0], held.at[v], load_sem.at[v]).wait()
        unscale = jnp.full((TILE, nx), kap[v], jnp.float32)
        for step in range(PASSES):
            def emit(i, value, step=step):
                if step < PASSES - 1:
                    field[step % 2, i * TILE : (i + 1) * TILE, :] = value
                else:
                    value = value * unscale
                    send[v, 2 * i] = folded(value, False)
                    send[v, 2 * i + 1] = folded(value, True)

            advance(getters(v, step), emit)

        @pl.when(v == 0)
        def _():
            pl.semaphore_wait(barrier, n - 1 + has_up.astype(jnp.int32) + has_down.astype(jnp.int32))

            @pl.when(has_up)
            def _():
                to_up().start()

            @pl.when(has_down)
            def _():
                to_down().start()

        @pl.when(v < vols - 1)
        def _():
            def whole(to):
                @pl.when(jnp.logical_and(to > 0, to < n - 1))
                def _():
                    sending(v, 0, depth, v, to).start()

            order(whole)

        @pl.when(v == vols - 1)
        def _():
            for p in range(parts):
                def part(to):
                    @pl.when(jnp.logical_and(to > 0, to < n - 1))
                    def _():
                        sending(v, p * PACK, PACK, vols - 1 + p, to).start()

                order(part)

    def edge(own, other, own_first, v):
        both = [own, other] if own_first else [other, own]
        for step in range(PASSES):
            made = []
            advance([lambda x=x: x for x in both], lambda i, value: made.append(value))
            both = made
        return both[0 if own_first else 1] * jnp.full(own.shape, kap[v], jnp.float32)

    @pl.when(has_up)
    def _():
        to_down().wait_recv()
        @pl.loop(0, vols)
        def _(v):
            beyond = scaled(halo[0, v], v)[PACK - TILE :]
            mine = scaled(held[v, :PACK, :], v)[:TILE]
            send[v, 0] = folded(edge(mine, beyond, False, v), False)

    @pl.when(has_down)
    def _():
        to_up().wait_recv()
        @pl.loop(0, vols)
        def _(v):
            beyond = scaled(halo[1, v], v)[:TILE]
            mine = scaled(held[v, rows - PACK : rows, :], v)[PACK - TILE :]
            send[v, n - 1] = folded(edge(mine, beyond, True, v), True)

    for to in (0, n - 1):
        @pl.when(me != to)
        def _():
            for piece in range(len(pieces)):
                sending(*pieces[piece], piece, to).start()

    own = [pltpu.make_async_copy(send.at[v, me], recv.at[me * vols + v], own_sem.at[v]) for v in range(vols)]
    for copy in own:
        copy.start()

    column = lax.broadcasted_iota(jnp.int32, (PACK, times * PACK), 1)
    diagonal = column % PACK == lax.broadcasted_iota(jnp.int32, (PACK, times * PACK), 0)
    source = column // PACK

    @pl.loop(0, times)
    def _(t):
        ahead = jnp.maximum(BAND - t, 0)
        behind = jnp.maximum(t + BAND + 1 - times, 0)
        total = (BAND + 1) ** 2 - (ahead * (ahead + 1) + behind * (behind + 1)) // 2
        raw = jnp.maximum(BAND + 1 - jnp.abs(source - t), 0).astype(jnp.float32)
        weight = raw / jnp.full(raw.shape, total, jnp.int32).astype(jnp.float32)
        mix[pl.ds(pl.multiple_of(t * PACK, PACK), PACK), :] = jnp.where(diagonal, weight, 0.0).astype(jnp.bfloat16)

    for copy in own:
        copy.wait()
    for piece in range(vols - 1):
        all_of(piece).wait_recv()

    block = min(times, 32)
    for p in range(parts):
        all_of(vols - 1 + p).wait_recv()
        span = slice(p * PACK, (p + 1) * PACK)
        values = recv[:, span, :].reshape(times * PACK, LANES)
        for start in range(0, times, block):
            these = pl.ds(start, block)
            base = jnp.dot(mix[start * PACK : (start + block) * PACK, :], values, preferred_element_type=jnp.float32)
            base = base.reshape(block, PACK, LANES)
            got = (recv[these, span, :].astype(jnp.float32) - base) * inverse(base + 0.1)
            ratio[these, span, :] = got
            dff[these, span, :] = got.astype(jnp.bfloat16)
        slope[0, span] = (ratio[1, span] - ratio[0, span]).astype(jnp.bfloat16)
        slope[1 : times - 1, span] = ((ratio[2:, span] - ratio[: times - 2, span]) * 0.5).astype(jnp.bfloat16)
        slope[times - 1, span] = (ratio[times - 1, span] - ratio[times - 2, span]).astype(jnp.bfloat16)

    for piece in range(len(pieces)):
        all_of(piece).wait_send()

    @pl.when(has_up)
    def _():
        to_up().wait_send()

    @pl.when(has_down)
    def _():
        to_down().wait_send()


def leave(dff, slope, dff_out, slope_out, sem):
    half = dff.shape[0] // 2
    copies = [
        pltpu.make_async_copy(source.at[pl.ds(h * half, half)], target.at[pl.ds(h * half, half)], sem.at[k, h])
        for k, (source, target) in enumerate(((dff, dff_out), (slope, slope_out)))
        for h in range(2)
    ]
    for copy in copies:
        copy.start()
    for copy in copies:
        copy.wait()


def local(n, strips, frames, kappa):
    vols, planes, rows, nx = frames.shape
    times = vols * n
    each = rows // n
    assert planes == 1 and each * 2 == TILE and nx % (2 * LANES) == 0
    depth = each * nx // LANES
    pieces = vols - 1 + depth // PACK
    out = jax.ShapeDtypeStruct((times, depth, LANES), jnp.bfloat16)
    f32, bf16 = jnp.float32, jnp.bfloat16
    results = pl.pallas_call(
        functools.partial(kernel, n, strips),
        out_shape=(out, out),
        in_specs=[pl.BlockSpec(memory_space=pltpu.HBM)] * 2,
        out_specs=(pl.BlockSpec(memory_space=pltpu.VMEM),) * 2,
        scratch_shapes=[
            pltpu.VMEM((vols, rows, nx), bf16),
            pltpu.SMEM((vols,), f32),
            pltpu.VMEM((2, vols, PACK, nx), bf16),
            pltpu.VMEM((2, rows, nx), f32),
            pltpu.VMEM((vols, n, depth, LANES), bf16),
            pltpu.VMEM((times, depth, LANES), bf16),
            pltpu.VMEM((times * PACK, times * PACK), bf16),
            pltpu.VMEM((times, depth, LANES), f32),
            pltpu.SemaphoreType.DMA((vols + 1,)),
            pltpu.SemaphoreType.DMA((2,)),
            pltpu.SemaphoreType.DMA((2,)),
            pltpu.SemaphoreType.DMA((pieces,)),
            pltpu.SemaphoreType.DMA((pieces,)),
            pltpu.SemaphoreType.DMA((vols,)),
        ],
        compiler_params=pltpu.CompilerParams(
            collective_id=0, has_side_effects=True, vmem_limit_bytes=40 * 1024 * 1024),
        cost_estimate=pl.CostEstimate(flops=200_000_000, bytes_accessed=1_000_000, transcendentals=1_000_000),
    )(pltpu.with_memory_space_constraint(frames, pltpu.HBM), pltpu.with_memory_space_constraint(kappa, pltpu.HBM))

    results = pl.pallas_call(
        leave,
        out_shape=(out, out),
        in_specs=[pl.BlockSpec(memory_space=pl.ANY)] * 2,
        out_specs=(pl.BlockSpec(memory_space=pltpu.HBM),) * 2,
        scratch_shapes=[pltpu.SemaphoreType.DMA((2, 2))],
        cost_estimate=pl.CostEstimate(flops=0, bytes_accessed=1_000_000, transcendentals=0),
    )(*results)

    def laid(value):
        value = value.reshape(times, nx // LANES, each, LANES).transpose(0, 2, 1, 3)
        return value.reshape(times, 1, each, 1, nx)

    return laid(results[0]), laid(results[1])


def solution(mesh):
    placed = P(None, None, "vol", "strip", None)
    return jax.shard_map(
        functools.partial(local, mesh.shape["vol"], mesh.shape["strip"]),
        mesh=mesh,
        in_specs=(P("vol", None, "strip", None), P("vol")),
        out_specs=(placed, placed),
        check_vma=False,
    )
```

```python
import functools

import jax
import jax.numpy as jnp
from jax import lax
from jax.experimental import pallas as pl
from jax.experimental.pallas import tpu as pltpu
from jax.sharding import PartitionSpec as P

PASSES = 3
BAND = 16
LANES = 128
TILE = 8
PACK = 16
MESH = pl.DeviceIdType.MESH


def inverse(value):
    guess = pltpu.reciprocal(value, approx=True)
    return guess * (2.0 - value * guess)


def flux(diff):
    return diff * inverse(1.0 + diff * diff)


def shifted_rows(center, below):
    row = lax.broadcasted_iota(jnp.int32, center.shape, 0)
    return pltpu.roll(jnp.where(row == 0, below, center), TILE - 1, 0)


def flux_x(center):
    nx = center.shape[1]
    lane = lax.broadcasted_iota(jnp.int32, (TILE, LANES), 1)
    left = pltpu.roll(center, 1, 1)
    left = jnp.concatenate([jnp.where(lane == 0, 0.0, left[:, :LANES]), left[:, LANES:]], axis=1)
    into = flux(left - center)
    out = pltpu.roll(into, nx - 1, 1)
    edge = flux(center[:, nx - LANES :])
    out = jnp.concatenate([out[:, : nx - LANES], jnp.where(lane == LANES - 1, edge, out[:, nx - LANES :])], axis=1)
    return into - out


def advance(tiles, emit):
    count = len(tiles)
    center = tiles[0]()
    zero = jnp.zeros_like(center)
    row = lax.broadcasted_iota(jnp.int32, center.shape, 0)
    before = flux(shifted_rows(zero, center))
    for i in range(count):
        below = tiles[i + 1]() if i + 1 < count else zero
        down = flux(shifted_rows(center, below) - center)
        up = pltpu.roll(jnp.where(row == TILE - 1, before, down), 1, 0)
        total = (down - up) + flux_x(center)
        emit(i, center + 0.2 * total)
        before, center = down, below


def folded(value, lower):
    small = lax.broadcasted_iota(jnp.int32, (TILE, LANES), 0) < TILE // 2
    swapped = pltpu.roll(value, TILE // 2, 0)
    first, second = (swapped, value) if lower else (value, swapped)
    parts = []
    for c in range(0, value.shape[1], 2 * LANES):
        parts.append(jnp.where(small, first[:, c : c + LANES], second[:, c + LANES : c + 2 * LANES]))
    return jnp.concatenate(parts, axis=0).astype(jnp.bfloat16)


def kernel(n, strips, frames, kappa, dff, slope, held, kap, rim, halo, beyond, field, send, recv, mix, ratio,
           load_sem, halo_send, halo_recv, send_sem, recv_sem, own_sem):
    vols, _, rows, nx = frames.shape
    times, depth, _ = recv.shape
    tiles = rows // TILE
    me = lax.axis_index("vol")
    strip = lax.axis_index("strip")
    has_up = strip > 0
    has_down = strip < strips - 1

    loads = [pltpu.make_async_copy(frames.at[v, 0], held.at[v], load_sem.at[v]) for v in range(vols)]
    load_kappa = pltpu.make_async_copy(kappa, kap, load_sem.at[vols])
    load_kappa.start()
    for load in loads:
        load.start()

    barrier = pltpu.get_barrier_semaphore()

    @pl.loop(1, n)
    def _(k):
        pl.semaphore_signal(barrier, inc=1, device_id={"vol": lax.rem(me + k, n)}, device_id_type=MESH)

    @pl.when(has_up)
    def _():
        pl.semaphore_signal(barrier, inc=1, device_id={"strip": strip - 1}, device_id_type=MESH)

    @pl.when(has_down)
    def _():
        pl.semaphore_signal(barrier, inc=1, device_id={"strip": strip + 1}, device_id_type=MESH)

    def to_up():
        return pltpu.make_async_remote_copy(
            src_ref=rim.at[1], dst_ref=halo.at[1], send_sem=halo_send.at[1], recv_sem=halo_recv.at[1],
            device_id={"strip": strip - 1}, device_id_type=MESH)

    def to_down():
        return pltpu.make_async_remote_copy(
            src_ref=rim.at[0], dst_ref=halo.at[0], send_sem=halo_send.at[0], recv_sem=halo_recv.at[0],
            device_id={"strip": strip + 1}, device_id_type=MESH)

    parts = depth // PACK
    pieces = [(v, 0, depth) for v in range(vols - 1)] + [(vols - 1, p * PACK, PACK) for p in range(parts)]

    def sending(v, start, length, piece, to):
        return pltpu.make_async_remote_copy(
            src_ref=send.at[v, to, pl.ds(start, length)], dst_ref=recv.at[me * vols + v, pl.ds(start, length)],
            send_sem=send_sem.at[piece], recv_sem=recv_sem.at[piece],
            device_id={"vol": to}, device_id_type=MESH)

    def all_of(piece):
        _, start, length = pieces[piece]
        return pltpu.make_async_remote_copy(
            src_ref=send.at[0, pl.ds(0, n - 1), pl.ds(start, length)], dst_ref=recv.at[pl.ds(0, n - 1), pl.ds(start, length)],
            send_sem=send_sem.at[piece], recv_sem=recv_sem.at[piece],
            device_id={"vol": lax.rem(me + 1, n)}, device_id_type=MESH)

    def scaled(block, v):
        return block.astype(jnp.float32) * (1.0 / jnp.full(block.shape, kap[v], jnp.float32))

    def getters(v, step):
        if step == 0:
            cache = {}

            def get(i):
                if i // 2 not in cache:
                    cache[i // 2] = scaled(held[v, (i // 2) * PACK : (i // 2 + 1) * PACK, :], v)
                return cache[i // 2][i % 2 * TILE : i % 2 * TILE + TILE]
        else:
            def get(i):
                return field[(step - 1) % 2, i * TILE : (i + 1) * TILE, :]
        return [functools.partial(get, i) for i in range(tiles)]

    def ready(to):
        return jnp.logical_not(jnp.logical_or(
            jnp.logical_and(has_up, to == 0), jnp.logical_and(has_down, to == n - 1)))

    def order(body):
        def step(j, _):
            away = (j + 1) // 2
            body(lax.rem(me + n // 2 + n + jnp.where(j % 2 == 1, away, -away), n))
            return _

        lax.fori_loop(0, n - 1, step, 0, unroll=n <= 16)

    load_kappa.wait()

    for load in loads:
        load.wait()

    f32 = jnp.float32
    rim[1] = jnp.concatenate(
        [held[v, :PACK, :].astype(f32)[:TILE] for v in range(vols)], axis=0).astype(jnp.bfloat16)
    rim[0] = jnp.concatenate(
        [held[v, rows - PACK :, :].astype(f32)[TILE:] for v in range(vols)], axis=0).astype(jnp.bfloat16)

    @pl.loop(0, vols)
    def _(v):
        unscale = jnp.full((TILE, nx), kap[v], jnp.float32)
        for step in range(PASSES):
            def emit(i, value, step=step):
                if step < PASSES - 1:
                    field[step % 2, i * TILE : (i + 1) * TILE, :] = value
                else:
                    value = value * unscale
                    send[v, 2 * i] = folded(value, False)
                    send[v, 2 * i + 1] = folded(value, True)

            advance(getters(v, step), emit)

            if step == 0:
                @pl.when(v == 0)
                def _():
                    pl.semaphore_wait(barrier, n - 1 + has_up.astype(jnp.int32) + has_down.astype(jnp.int32))

                    @pl.when(has_up)
                    def _():
                        to_up().start()

                    @pl.when(has_down)
                    def _():
                        to_down().start()

        @pl.when(v < vols - 1)
        def _():
            def whole(to):
                @pl.when(ready(to))
                def _():
                    sending(v, 0, depth, v, to).start()

            order(whole)

        @pl.when(v == vols - 1)
        def _():
            for p in range(parts):
                def part(to):
                    @pl.when(ready(to))
                    def _():
                        sending(v, p * PACK, PACK, vols - 1 + p, to).start()

                order(part)

    def edge(own, other, own_first, v):
        both = [own, other] if own_first else [other, own]
        for step in range(PASSES):
            made = []
            advance([lambda x=x: x for x in both], lambda i, value: made.append(value))
            both = made
        return both[0 if own_first else 1] * jnp.full(own.shape, kap[v], jnp.float32)

    def edges(to, copy, which, own_first):
        copy.wait_recv()
        got = halo[which].astype(f32)
        for v in range(vols):
            beyond[v] = got[v * TILE : (v + 1) * TILE]

        @pl.loop(0, vols)
        def _(v):
            other = scaled(beyond[v], v)
            if own_first:
                mine = scaled(held[v, rows - PACK : rows, :], v)[TILE:]
            else:
                mine = scaled(held[v, :PACK, :], v)[:TILE]
            send[v, to] = folded(edge(mine, other, own_first, v), own_first)

        @pl.when(me != to)
        def _():
            for piece in range(len(pieces)):
                sending(*pieces[piece], piece, to).start()

    @pl.when(has_up)
    def _():
        edges(0, to_down(), 0, False)

    @pl.when(has_down)
    def _():
        edges(n - 1, to_up(), 1, True)

    own = [pltpu.make_async_copy(send.at[v, me], recv.at[me * vols + v], own_sem.at[v]) for v in range(vols)]
    for copy in own:
        copy.start()

    column = lax.broadcasted_iota(jnp.int32, (PACK, times * PACK), 1)
    diagonal = column % PACK == lax.broadcasted_iota(jnp.int32, (PACK, times * PACK), 0)
    source = column // PACK

    @pl.loop(0, times)
    def _(t):
        ahead = jnp.maximum(BAND - t, 0)
        behind = jnp.maximum(t + BAND + 1 - times, 0)
        total = (BAND + 1) ** 2 - (ahead * (ahead + 1) + behind * (behind + 1)) // 2
        raw = jnp.maximum(BAND + 1 - jnp.abs(source - t), 0).astype(jnp.float32)
        weight = raw / jnp.full(raw.shape, total, jnp.int32).astype(jnp.float32)
        mix[pl.ds(pl.multiple_of(t * PACK, PACK), PACK), :] = jnp.where(diagonal, weight, 0.0).astype(jnp.bfloat16)

    for copy in own:
        copy.wait()
    for piece in range(vols - 1):
        all_of(piece).wait_recv()

    block = min(times, 32)
    for p in range(parts):
        all_of(vols - 1 + p).wait_recv()
        span = slice(p * PACK, (p + 1) * PACK)
        values = recv[:, span, :].reshape(times * PACK, LANES)
        for start in range(0, times, block):
            these = pl.ds(start, block)
            base = jnp.dot(mix[start * PACK : (start + block) * PACK, :], values, preferred_element_type=jnp.float32)
            base = base.reshape(block, PACK, LANES)
            got = (recv[these, span, :].astype(jnp.float32) - base) * inverse(base + 0.1)
            ratio[these, span, :] = got
            dff[these, span, :] = got.astype(jnp.bfloat16)
        slope[0, span] = (ratio[1, span] - ratio[0, span]).astype(jnp.bfloat16)
        slope[1 : times - 1, span] = ((ratio[2:, span] - ratio[: times - 2, span]) * 0.5).astype(jnp.bfloat16)
        slope[times - 1, span] = (ratio[times - 1, span] - ratio[times - 2, span]).astype(jnp.bfloat16)

    for piece in range(len(pieces)):
        all_of(piece).wait_send()

    @pl.when(has_up)
    def _():
        to_up().wait_send()

    @pl.when(has_down)
    def _():
        to_down().wait_send()


def leave(dff, slope, dff_out, slope_out, sem):
    half = dff.shape[0] // 2
    copies = [
        pltpu.make_async_copy(source.at[pl.ds(h * half, half)], target.at[pl.ds(h * half, half)], sem.at[k, h])
        for k, (source, target) in enumerate(((dff, dff_out), (slope, slope_out)))
        for h in range(2)
    ]
    for copy in copies:
        copy.start()
    for copy in copies:
        copy.wait()


def local(n, strips, frames, kappa):
    vols, planes, rows, nx = frames.shape
    times = vols * n
    each = rows // n
    assert planes == 1 and each * 2 == TILE and nx % (2 * LANES) == 0
    depth = each * nx // LANES
    pieces = vols - 1 + depth // PACK
    out = jax.ShapeDtypeStruct((times, depth, LANES), jnp.bfloat16)
    f32, bf16 = jnp.float32, jnp.bfloat16
    results = pl.pallas_call(
        functools.partial(kernel, n, strips),
        out_shape=(out, out),
        in_specs=[pl.BlockSpec(memory_space=pltpu.HBM)] * 2,
        out_specs=(pl.BlockSpec(memory_space=pltpu.VMEM),) * 2,
        scratch_shapes=[
            pltpu.VMEM((vols, rows, nx), bf16),
            pltpu.SMEM((vols,), f32),
            pltpu.VMEM((2, vols * TILE, nx), bf16),
            pltpu.VMEM((2, vols * TILE, nx), bf16),
            pltpu.VMEM((vols, TILE, nx), f32),
            pltpu.VMEM((2, rows, nx), f32),
            pltpu.VMEM((vols, n, depth, LANES), bf16),
            pltpu.VMEM((times, depth, LANES), bf16),
            pltpu.VMEM((times * PACK, times * PACK), bf16),
            pltpu.VMEM((times, depth, LANES), f32),
            pltpu.SemaphoreType.DMA((vols + 1,)),
            pltpu.SemaphoreType.DMA((2,)),
            pltpu.SemaphoreType.DMA((2,)),
            pltpu.SemaphoreType.DMA((pieces,)),
            pltpu.SemaphoreType.DMA((pieces,)),
            pltpu.SemaphoreType.DMA((vols,)),
        ],
        compiler_params=pltpu.CompilerParams(
            collective_id=0, has_side_effects=True, vmem_limit_bytes=40 * 1024 * 1024),
        cost_estimate=pl.CostEstimate(flops=200_000_000, bytes_accessed=1_000_000, transcendentals=1_000_000),
    )(pltpu.with_memory_space_constraint(frames, pltpu.HBM), pltpu.with_memory_space_constraint(kappa, pltpu.HBM))

    results = pl.pallas_call(
        leave,
        out_shape=(out, out),
        in_specs=[pl.BlockSpec(memory_space=pl.ANY)] * 2,
        out_specs=(pl.BlockSpec(memory_space=pltpu.HBM),) * 2,
        scratch_shapes=[pltpu.SemaphoreType.DMA((2, 2))],
        compiler_params=pltpu.CompilerParams(vmem_limit_bytes=2 * 1024 * 1024),
        cost_estimate=pl.CostEstimate(flops=0, bytes_accessed=1_000_000, transcendentals=0),
    )(*[pltpu.with_memory_space_constraint(x, pltpu.VMEM) for x in results])

    def laid(value):
        value = value.reshape(times, nx // LANES, each, LANES).transpose(0, 2, 1, 3)
        return value.reshape(times, 1, each, 1, nx)

    return laid(results[0]), laid(results[1])


def solution(mesh):
    placed = P(None, None, "vol", "strip", None)
    return jax.shard_map(
        functools.partial(local, mesh.shape["vol"], mesh.shape["strip"]),
        mesh=mesh,
        in_specs=(P("vol", None, "strip", None), P("vol")),
        out_specs=(placed, placed),
        check_vma=False,
    )
```

```python
import functools

import jax
import jax.numpy as jnp
from jax import lax
from jax.experimental import pallas as pl
from jax.experimental.pallas import tpu as pltpu
from jax.sharding import PartitionSpec as P

PASSES = 3
BAND = 16
LANES = 128
TILE = 8
PACK = 16
MESH = pl.DeviceIdType.MESH


def inverse(value):
    guess = pltpu.reciprocal(value, approx=True)
    return guess * (2.0 - value * guess)


def flux(diff):
    return diff * inverse(1.0 + diff * diff)


def shifted_rows(center, below):
    row = lax.broadcasted_iota(jnp.int32, center.shape, 0)
    return pltpu.roll(jnp.where(row == 0, below, center), TILE - 1, 0)


def flux_x(center):
    nx = center.shape[1]
    lane = lax.broadcasted_iota(jnp.int32, (TILE, LANES), 1)
    left = pltpu.roll(center, 1, 1)
    left = jnp.concatenate([jnp.where(lane == 0, 0.0, left[:, :LANES]), left[:, LANES:]], axis=1)
    into = flux(left - center)
    out = pltpu.roll(into, nx - 1, 1)
    edge = flux(center[:, nx - LANES :])
    out = jnp.concatenate([out[:, : nx - LANES], jnp.where(lane == LANES - 1, edge, out[:, nx - LANES :])], axis=1)
    return into - out


def advance(above, tiles, below, emit):
    center = tiles[0]()
    row = lax.broadcasted_iota(jnp.int32, center.shape, 0)
    before = above()
    before = flux(shifted_rows(before, center) - before)
    for i in range(len(tiles)):
        after = tiles[i + 1]() if i + 1 < len(tiles) else below()
        down = flux(shifted_rows(center, after) - center)
        up = pltpu.roll(jnp.where(row == TILE - 1, before, down), 1, 0)
        total = (down - up) + flux_x(center)
        emit(i, center + 0.2 * total)
        before, center = down, after


def folded(value, lower):
    small = lax.broadcasted_iota(jnp.int32, (TILE, LANES), 0) < TILE // 2
    swapped = pltpu.roll(value, TILE // 2, 0)
    first, second = (swapped, value) if lower else (value, swapped)
    parts = []
    for c in range(0, value.shape[1], 2 * LANES):
        parts.append(jnp.where(small, first[:, c : c + LANES], second[:, c + LANES : c + 2 * LANES]))
    return jnp.concatenate(parts, axis=0).astype(jnp.bfloat16)


def kernel(n, strips, frames, kappa, dff, slope, held, kap, rim, halo, beyond, start, field, send, recv, mix, ratio,
           load_sem, halo_send, halo_recv, send_sem, recv_sem, own_sem):
    vols, _, rows, nx = frames.shape
    times, depth, _ = recv.shape
    tiles = rows // TILE
    me = lax.axis_index("vol")
    strip = lax.axis_index("strip")
    has_up = strip > 0
    has_down = strip < strips - 1

    loads = [pltpu.make_async_copy(frames.at[v, 0], held.at[v], load_sem.at[v]) for v in range(vols)]
    load_kappa = pltpu.make_async_copy(kappa, kap, load_sem.at[vols])
    load_kappa.start()
    for load in loads:
        load.start()

    barrier = pltpu.get_barrier_semaphore()

    @pl.loop(1, n)
    def _(k):
        pl.semaphore_signal(barrier, inc=1, device_id={"vol": lax.rem(me + k, n)}, device_id_type=MESH)

    @pl.when(has_up)
    def _():
        pl.semaphore_signal(barrier, inc=1, device_id={"strip": strip - 1}, device_id_type=MESH)

    @pl.when(has_down)
    def _():
        pl.semaphore_signal(barrier, inc=1, device_id={"strip": strip + 1}, device_id_type=MESH)

    def to_up():
        return pltpu.make_async_remote_copy(
            src_ref=rim.at[1], dst_ref=halo.at[1], send_sem=halo_send.at[1], recv_sem=halo_recv.at[1],
            device_id={"strip": strip - 1}, device_id_type=MESH)

    def to_down():
        return pltpu.make_async_remote_copy(
            src_ref=rim.at[0], dst_ref=halo.at[0], send_sem=halo_send.at[0], recv_sem=halo_recv.at[0],
            device_id={"strip": strip + 1}, device_id_type=MESH)

    parts = depth // PACK
    group = n // 2
    side = me // group
    near, first_part = vols - 1, vols

    def sending(v, start, length, piece, to):
        return pltpu.make_async_remote_copy(
            src_ref=send.at[v, to, pl.ds(start, length)], dst_ref=recv.at[me * vols + v, pl.ds(start, length)],
            send_sem=send_sem.at[piece], recv_sem=recv_sem.at[piece],
            device_id={"vol": to}, device_id_type=MESH)

    def all_of(piece):
        count, length = n - 1, depth
        if piece == near:
            count = group - 1
        elif piece >= first_part:
            count, length = group, PACK
        return pltpu.make_async_remote_copy(
            src_ref=send.at[0, pl.ds(0, count), pl.ds(0, length)], dst_ref=recv.at[pl.ds(0, count), pl.ds(0, length)],
            send_sem=send_sem.at[piece], recv_sem=recv_sem.at[piece],
            device_id={"vol": lax.rem(me + 1, n)}, device_id_type=MESH)

    def scaled(block, v):
        return block.astype(jnp.float32) * (1.0 / jnp.full(block.shape, kap[v], jnp.float32))

    def tile(ref, i):
        return ref[pl.ds(pl.multiple_of(i * TILE, TILE), TILE), :]

    def getters(ref, start, count):
        return [functools.partial(tile, ref, start + i) for i in range(count)]

    def ready(to):
        return jnp.logical_not(jnp.logical_or(
            jnp.logical_or(jnp.logical_and(has_up, to == 0), jnp.logical_and(has_down, to == n - 1)), to == me))

    zero = jnp.zeros((TILE, nx), jnp.float32)
    some = tiles // 2
    for buffer in (0, 1):
        field[buffer, :TILE, :] = zero
        field[buffer, (some + 2) * TILE :, :] = zero
    for v in range(vols):
        start[v, :TILE, :] = zero
        start[v, (tiles + 1) * TILE :, :] = zero

    load_kappa.wait()
    for load in loads:
        load.wait()

    f32 = jnp.float32
    rim[1] = jnp.concatenate(
        [held[v, :PACK, :].astype(f32)[:TILE] for v in range(vols)], axis=0).astype(jnp.bfloat16)
    rim[0] = jnp.concatenate(
        [held[v, rows - PACK :, :].astype(f32)[TILE:] for v in range(vols)], axis=0).astype(jnp.bfloat16)
    for v in range(vols):
        for i in range(rows // PACK):
            start[v, TILE + i * PACK : TILE + (i + 1) * PACK, :] = scaled(held[v, i * PACK : (i + 1) * PACK, :], v)

    @pl.loop(0, 2 * vols)
    def _(unit):
        v = lax.rem(unit, vols)
        away = unit < vols
        half = jnp.where(away, 1 - side, side)
        unscale = jnp.full((TILE, nx), kap[v], jnp.float32)

        def keep(buffer):
            def emit(i, value):
                field[buffer, (i + 1) * TILE : (i + 2) * TILE, :] = value
            return emit

        def pack(i, value):
            value = value * unscale
            to = half * group + 2 * i
            send[v, to] = folded(value, False)
            send[v, to + 1] = folded(value, True)

        base = half * (some - 1)
        source = start.at[v]
        get = getters(source, base, some + 3)
        advance(get[0], get[1:-1], get[-1], keep(0))
        get = getters(field.at[0], 0, some + 3)
        advance(get[0], get[1:-1], get[-1], keep(1))
        get = getters(field.at[1], half, some + 2)
        advance(get[0], get[1:-1], get[-1], pack)

        @pl.when(unit == 0)
        def _():
            pl.semaphore_wait(barrier, n - 1 + has_up.astype(jnp.int32) + has_down.astype(jnp.int32))

            @pl.when(has_up)
            def _():
                to_up().start()

            @pl.when(has_down)
            def _():
                to_down().start()

        def each(first, length, piece):
            def step(j, _):
                to = half * group + lax.rem(me + j, group)

                @pl.when(ready(to))
                def _():
                    sending(v, first, length, piece, to).start()

                return 0

            lax.fori_loop(0, group, step, 0, unroll=group <= 8)

        last = v == vols - 1

        @pl.when(jnp.logical_not(jnp.logical_and(last, away)))
        def _():
            each(0, depth, v)

        @pl.when(jnp.logical_and(last, away))
        def _():
            for p in range(parts):
                each(p * PACK, PACK, first_part + p)

    def edge(own, other, own_first, v):
        both = [own, other] if own_first else [other, own]
        for step in range(PASSES):
            made = []
            outside = lambda: jnp.zeros_like(own)
            advance(outside, [lambda x=x: x for x in both], outside, lambda i, value: made.append(value))
            both = made
        return both[0 if own_first else 1] * jnp.full(own.shape, kap[v], jnp.float32)

    def edges(to, copy, which, own_first):
        copy.wait_recv()
        got = halo[which].astype(f32)
        for v in range(vols):
            beyond[v] = got[v * TILE : (v + 1) * TILE]

        @pl.loop(0, vols)
        def _(v):
            other = scaled(beyond[v], v)
            at = tiles if own_first else 1
            mine = start[v, at * TILE : (at + 1) * TILE, :]
            send[v, to] = folded(edge(mine, other, own_first, v), own_first)

        same = side == to // group

        @pl.when(me != to)
        def _():
            for v in range(vols - 1):
                sending(v, 0, depth, v, to).start()

            @pl.when(same)
            def _():
                sending(vols - 1, 0, depth, near, to).start()

            @pl.when(jnp.logical_not(same))
            def _():
                for p in range(parts):
                    sending(vols - 1, p * PACK, PACK, first_part + p, to).start()

    @pl.when(has_up)
    def _():
        edges(0, to_down(), 0, False)

    @pl.when(has_down)
    def _():
        edges(n - 1, to_up(), 1, True)

    own = [pltpu.make_async_copy(send.at[v, me], recv.at[me * vols + v], own_sem.at[v]) for v in range(vols)]
    for copy in own:
        copy.start()

    column = lax.broadcasted_iota(jnp.int32, (PACK, times * PACK), 1)
    diagonal = column % PACK == lax.broadcasted_iota(jnp.int32, (PACK, times * PACK), 0)
    source = column // PACK

    @pl.loop(0, times)
    def _(t):
        ahead = jnp.maximum(BAND - t, 0)
        behind = jnp.maximum(t + BAND + 1 - times, 0)
        total = (BAND + 1) ** 2 - (ahead * (ahead + 1) + behind * (behind + 1)) // 2
        raw = jnp.maximum(BAND + 1 - jnp.abs(source - t), 0).astype(jnp.float32)
        weight = raw / jnp.full(raw.shape, total, jnp.int32).astype(jnp.float32)
        mix[pl.ds(pl.multiple_of(t * PACK, PACK), PACK), :] = jnp.where(diagonal, weight, 0.0).astype(jnp.bfloat16)

    for copy in own:
        copy.wait()
    for piece in range(vols):
        all_of(piece).wait_recv()

    block = min(times, 32)
    for p in range(parts):
        all_of(first_part + p).wait_recv()
        span = slice(p * PACK, (p + 1) * PACK)
        values = recv[:, span, :].reshape(times * PACK, LANES)
        for t in range(0, times, block):
            these = pl.ds(t, block)
            base = jnp.dot(mix[t * PACK : (t + block) * PACK, :], values, preferred_element_type=jnp.float32)
            base = base.reshape(block, PACK, LANES)
            got = (recv[these, span, :].astype(jnp.float32) - base) * inverse(base + 0.1)
            ratio[these, span, :] = got
            dff[these, span, :] = got.astype(jnp.bfloat16)
        slope[0, span] = (ratio[1, span] - ratio[0, span]).astype(jnp.bfloat16)
        slope[1 : times - 1, span] = ((ratio[2:, span] - ratio[: times - 2, span]) * 0.5).astype(jnp.bfloat16)
        slope[times - 1, span] = (ratio[times - 1, span] - ratio[times - 2, span]).astype(jnp.bfloat16)

    for piece in range(vols + parts):
        all_of(piece).wait_send()

    @pl.when(has_up)
    def _():
        to_up().wait_send()

    @pl.when(has_down)
    def _():
        to_down().wait_send()


def leave(dff, slope, dff_out, slope_out, sem):
    half = dff.shape[0] // 2
    copies = [
        pltpu.make_async_copy(source.at[pl.ds(h * half, half)], target.at[pl.ds(h * half, half)], sem.at[k, h])
        for k, (source, target) in enumerate(((dff, dff_out), (slope, slope_out)))
        for h in range(2)
    ]
    for copy in copies:
        copy.start()
    for copy in copies:
        copy.wait()


def local(n, strips, frames, kappa):
    vols, planes, rows, nx = frames.shape
    times = vols * n
    each = rows // n
    assert planes == 1 and each * 2 == TILE and nx % (2 * LANES) == 0
    depth = each * nx // LANES
    pieces = vols + depth // PACK
    out = jax.ShapeDtypeStruct((times, depth, LANES), jnp.bfloat16)
    f32, bf16 = jnp.float32, jnp.bfloat16
    results = pl.pallas_call(
        functools.partial(kernel, n, strips),
        out_shape=(out, out),
        in_specs=[pl.BlockSpec(memory_space=pltpu.HBM)] * 2,
        out_specs=(pl.BlockSpec(memory_space=pltpu.VMEM),) * 2,
        scratch_shapes=[
            pltpu.VMEM((vols, rows, nx), bf16),
            pltpu.SMEM((vols,), f32),
            pltpu.VMEM((2, vols * TILE, nx), bf16),
            pltpu.VMEM((2, vols * TILE, nx), bf16),
            pltpu.VMEM((vols, TILE, nx), f32),
            pltpu.VMEM((vols, rows + 2 * TILE, nx), f32),
            pltpu.VMEM((2, rows // 2 + 3 * TILE, nx), f32),
            pltpu.VMEM((vols, n, depth, LANES), bf16),
            pltpu.VMEM((times, depth, LANES), bf16),
            pltpu.VMEM((times * PACK, times * PACK), bf16),
            pltpu.VMEM((times, depth, LANES), f32),
            pltpu.SemaphoreType.DMA((vols + 1,)),
            pltpu.SemaphoreType.DMA((2,)),
            pltpu.SemaphoreType.DMA((2,)),
            pltpu.SemaphoreType.DMA((pieces,)),
            pltpu.SemaphoreType.DMA((pieces,)),
            pltpu.SemaphoreType.DMA((vols,)),
        ],
        compiler_params=pltpu.CompilerParams(
            collective_id=0, has_side_effects=True, vmem_limit_bytes=40 * 1024 * 1024),
        cost_estimate=pl.CostEstimate(flops=200_000_000, bytes_accessed=1_000_000, transcendentals=1_000_000),
    )(pltpu.with_memory_space_constraint(frames, pltpu.HBM), pltpu.with_memory_space_constraint(kappa, pltpu.HBM))

    results = pl.pallas_call(
        leave,
        out_shape=(out, out),
        in_specs=[pl.BlockSpec(memory_space=pl.ANY)] * 2,
        out_specs=(pl.BlockSpec(memory_space=pltpu.HBM),) * 2,
        scratch_shapes=[pltpu.SemaphoreType.DMA((2, 2))],
        compiler_params=pltpu.CompilerParams(vmem_limit_bytes=2 * 1024 * 1024),
        cost_estimate=pl.CostEstimate(flops=0, bytes_accessed=1_000_000, transcendentals=0),
    )(*[pltpu.with_memory_space_constraint(x, pltpu.VMEM) for x in results])

    def laid(value):
        value = value.reshape(times, nx // LANES, each, LANES).transpose(0, 2, 1, 3)
        return value.reshape(times, 1, each, 1, nx)

    return laid(results[0]), laid(results[1])


def solution(mesh):
    placed = P(None, None, "vol", "strip", None)
    return jax.shard_map(
        functools.partial(local, mesh.shape["vol"], mesh.shape["strip"]),
        mesh=mesh,
        in_specs=(P("vol", None, "strip", None), P("vol")),
        out_specs=(placed, placed),
        check_vma=False,
    )
```

```python
import functools

import jax
import jax.numpy as jnp
from jax import lax
from jax.experimental import pallas as pl
from jax.experimental.pallas import tpu as pltpu
from jax.sharding import PartitionSpec as P

PASSES = 3
BAND = 16
LANES = 128
TILE = 8
PACK = 16
MESH = pl.DeviceIdType.MESH


def inverse(value):
    guess = pltpu.reciprocal(value, approx=True)
    return guess * (2.0 - value * guess)


def flux(diff):
    return diff * inverse(1.0 + diff * diff)


def shifted_rows(center, below):
    row = lax.broadcasted_iota(jnp.int32, center.shape, 0)
    return pltpu.roll(jnp.where(row == 0, below, center), TILE - 1, 0)


def flux_x(center):
    nx = center.shape[1]
    lane = lax.broadcasted_iota(jnp.int32, (TILE, LANES), 1)
    left = pltpu.roll(center, 1, 1)
    left = jnp.concatenate([jnp.where(lane == 0, 0.0, left[:, :LANES]), left[:, LANES:]], axis=1)
    into = flux(left - center)
    out = pltpu.roll(into, nx - 1, 1)
    edge = flux(center[:, nx - LANES :])
    out = jnp.concatenate([out[:, : nx - LANES], jnp.where(lane == LANES - 1, edge, out[:, nx - LANES :])], axis=1)
    return into - out


def advance(above, tiles, below, emit):
    center = tiles[0]()
    row = lax.broadcasted_iota(jnp.int32, center.shape, 0)
    before = above()
    before = flux(shifted_rows(before, center) - before)
    for i in range(len(tiles)):
        after = tiles[i + 1]() if i + 1 < len(tiles) else below()
        down = flux(shifted_rows(center, after) - center)
        up = pltpu.roll(jnp.where(row == TILE - 1, before, down), 1, 0)
        total = (down - up) + flux_x(center)
        emit(i, center + 0.2 * total)
        before, center = down, after


def folded(value, lower):
    small = lax.broadcasted_iota(jnp.int32, (TILE, LANES), 0) < TILE // 2
    swapped = pltpu.roll(value, TILE // 2, 0)
    first, second = (swapped, value) if lower else (value, swapped)
    parts = []
    for c in range(0, value.shape[1], 2 * LANES):
        parts.append(jnp.where(small, first[:, c : c + LANES], second[:, c + LANES : c + 2 * LANES]))
    return jnp.concatenate(parts, axis=0).astype(jnp.bfloat16)


def kernel(n, strips, frames, kappa, dff, slope, held, kap, rim, halo, beyond, start, field, send, recv, mix, ratio,
           load_sem, halo_send, halo_recv, send_sem, recv_sem, own_sem):
    vols, _, rows, nx = frames.shape
    times, depth, _ = recv.shape
    tiles = rows // TILE
    me = lax.axis_index("vol")
    strip = lax.axis_index("strip")
    has_up = strip > 0
    has_down = strip < strips - 1

    loads = [pltpu.make_async_copy(frames.at[v, 0], held.at[v], load_sem.at[v]) for v in range(vols)]
    load_kappa = pltpu.make_async_copy(kappa, kap, load_sem.at[vols])
    load_kappa.start()
    for load in loads:
        load.start()

    barrier = pltpu.get_barrier_semaphore()

    @pl.loop(1, n)
    def _(k):
        pl.semaphore_signal(barrier, inc=1, device_id={"vol": lax.rem(me + k, n)}, device_id_type=MESH)

    @pl.when(has_up)
    def _():
        pl.semaphore_signal(barrier, inc=1, device_id={"strip": strip - 1}, device_id_type=MESH)

    @pl.when(has_down)
    def _():
        pl.semaphore_signal(barrier, inc=1, device_id={"strip": strip + 1}, device_id_type=MESH)

    def to_up():
        return pltpu.make_async_remote_copy(
            src_ref=rim.at[1], dst_ref=halo.at[1], send_sem=halo_send.at[1], recv_sem=halo_recv.at[1],
            device_id={"strip": strip - 1}, device_id_type=MESH)

    def to_down():
        return pltpu.make_async_remote_copy(
            src_ref=rim.at[0], dst_ref=halo.at[0], send_sem=halo_send.at[0], recv_sem=halo_recv.at[0],
            device_id={"strip": strip + 1}, device_id_type=MESH)

    parts = depth // PACK
    group = n // 2
    side = me // group
    near, first_part = vols - 1, vols

    def sending(v, start, length, piece, to):
        return pltpu.make_async_remote_copy(
            src_ref=send.at[v, to, pl.ds(start, length)], dst_ref=recv.at[me * vols + v, pl.ds(start, length)],
            send_sem=send_sem.at[piece], recv_sem=recv_sem.at[piece],
            device_id={"vol": to}, device_id_type=MESH)

    def joined(to):
        return pltpu.make_async_remote_copy(
            src_ref=send.at[:, to], dst_ref=recv.at[pl.ds(me * vols, vols)],
            send_sem=send_sem.at[near], recv_sem=recv_sem.at[near],
            device_id={"vol": to}, device_id_type=MESH)

    def all_of(piece):
        count = (group - 1) * vols if piece == near else group
        these = recv.at[pl.ds(0, count), pl.ds(0, PACK if piece >= first_part else depth)]
        return pltpu.make_async_remote_copy(
            src_ref=these, dst_ref=these, send_sem=send_sem.at[piece], recv_sem=recv_sem.at[piece],
            device_id={"vol": lax.rem(me + 1, n)}, device_id_type=MESH)

    def scaled(block, v):
        return block.astype(jnp.float32) * (1.0 / jnp.full(block.shape, kap[v], jnp.float32))

    def tile(ref, i):
        return ref[pl.ds(pl.multiple_of(i * TILE, TILE), TILE), :]

    def getters(ref, start, count):
        return [functools.partial(tile, ref, start + i) for i in range(count)]

    def ready(to):
        return jnp.logical_not(jnp.logical_or(
            jnp.logical_or(jnp.logical_and(has_up, to == 0), jnp.logical_and(has_down, to == n - 1)), to == me))

    zero = jnp.zeros((TILE, nx), jnp.float32)
    some = tiles // 2
    for buffer in (0, 1):
        field[buffer, :TILE, :] = zero
        field[buffer, (some + 2) * TILE :, :] = zero
    for v in range(vols):
        start[v, :TILE, :] = zero
        start[v, (tiles + 1) * TILE :, :] = zero

    column = lax.broadcasted_iota(jnp.int32, (PACK, times * PACK), 1)
    diagonal = column % PACK == lax.broadcasted_iota(jnp.int32, (PACK, times * PACK), 0)
    source = jnp.where(diagonal, column // PACK, -2 * times - BAND).astype(jnp.float32)

    def weigh(t, _):
        ahead = jnp.maximum(BAND - t, 0)
        behind = jnp.maximum(t + BAND + 1 - times, 0)
        total = (BAND + 1) ** 2 - (ahead * (ahead + 1) + behind * (behind + 1)) // 2
        share = 1.0 / jnp.full((TILE, LANES), total, jnp.int32).astype(jnp.float32)
        raw = jnp.maximum(BAND + 1 - jnp.abs(source - t.astype(jnp.float32)), 0.0)
        raw = raw.reshape(PACK // TILE, TILE, times * PACK)
        weight = jnp.concatenate(
            [raw[:, :, c : c + LANES] * share[None] for c in range(0, times * PACK, LANES)], axis=2)
        mix[pl.ds(pl.multiple_of(t * PACK, PACK), PACK), :] = weight.reshape(PACK, times * PACK).astype(jnp.bfloat16)
        return 0

    lax.fori_loop(0, times, weigh, 0, unroll=8)

    f32 = jnp.float32

    def enter(v):
        loads[v].wait()
        for i in range(rows // PACK):
            start[v, TILE + i * PACK : TILE + (i + 1) * PACK, :] = scaled(held[v, i * PACK : (i + 1) * PACK, :], v)

    load_kappa.wait()
    enter(0)

    @pl.loop(0, 2 * vols)
    def _(unit):
        v = lax.rem(unit, vols)
        away = unit < vols
        half = jnp.where(away, 1 - side, side)
        unscale = jnp.full((TILE, nx), kap[v], jnp.float32)

        def keep(buffer):
            def emit(i, value):
                field[buffer, (i + 1) * TILE : (i + 2) * TILE, :] = value
            return emit

        def pack(i, value):
            value = value * unscale
            to = half * group + 2 * i
            send[v, to] = folded(value, False)
            send[v, to + 1] = folded(value, True)

        base = half * (some - 1)
        source = start.at[v]
        get = getters(source, base, some + 3)
        advance(get[0], get[1:-1], get[-1], keep(0))
        get = getters(field.at[0], 0, some + 3)
        advance(get[0], get[1:-1], get[-1], keep(1))
        get = getters(field.at[1], half, some + 2)
        advance(get[0], get[1:-1], get[-1], pack)

        @pl.when(unit == 0)
        def _():
            for w in range(1, vols):
                enter(w)
            rim[1] = jnp.concatenate(
                [held[w, :PACK, :].astype(f32)[:TILE] for w in range(vols)], axis=0).astype(jnp.bfloat16)
            rim[0] = jnp.concatenate(
                [held[w, rows - PACK :, :].astype(f32)[TILE:] for w in range(vols)], axis=0).astype(jnp.bfloat16)
            pl.semaphore_wait(barrier, n - 1 + has_up.astype(jnp.int32) + has_down.astype(jnp.int32))

            @pl.when(has_up)
            def _():
                to_up().start()

            @pl.when(has_down)
            def _():
                to_down().start()

        def each(copy):
            def step(j, _):
                to = half * group + lax.rem(me + j, group)

                @pl.when(ready(to))
                def _():
                    copy(to).start()

                return 0

            lax.fori_loop(0, group, step, 0, unroll=group <= 8)

        last = v == vols - 1

        @pl.when(jnp.logical_and(away, jnp.logical_not(last)))
        def _():
            each(lambda to: sending(v, 0, depth, v, to))

        @pl.when(jnp.logical_and(away, last))
        def _():
            for p in range(parts):
                each(lambda to: sending(v, p * PACK, PACK, first_part + p, to))

        @pl.when(jnp.logical_and(last, jnp.logical_not(away)))
        def _():
            each(joined)

    def edge(own, other, own_first, v):
        both = [own, other] if own_first else [other, own]
        for step in range(PASSES):
            made = []
            outside = lambda: jnp.zeros_like(own)
            advance(outside, [lambda x=x: x for x in both], outside, lambda i, value: made.append(value))
            both = made
        return both[0 if own_first else 1] * jnp.full(own.shape, kap[v], jnp.float32)

    def edges(to, copy, which, own_first):
        copy.wait_recv()
        got = halo[which].astype(f32)
        for v in range(vols):
            beyond[v] = got[v * TILE : (v + 1) * TILE]

        @pl.loop(0, vols)
        def _(v):
            other = scaled(beyond[v], v)
            at = tiles if own_first else 1
            mine = start[v, at * TILE : (at + 1) * TILE, :]
            send[v, to] = folded(edge(mine, other, own_first, v), own_first)

        same = side == to // group

        @pl.when(jnp.logical_and(same, me != to))
        def _():
            joined(to).start()

        @pl.when(jnp.logical_not(same))
        def _():
            for v in range(vols - 1):
                sending(v, 0, depth, v, to).start()
            for p in range(parts):
                sending(vols - 1, p * PACK, PACK, first_part + p, to).start()

    @pl.when(has_up)
    def _():
        edges(0, to_down(), 0, False)

    @pl.when(has_down)
    def _():
        edges(n - 1, to_up(), 1, True)

    own = [pltpu.make_async_copy(send.at[v, me], recv.at[me * vols + v], own_sem.at[v]) for v in range(vols)]
    for copy in own:
        copy.start()

    for copy in own:
        copy.wait()
    for piece in range(vols):
        all_of(piece).wait_recv()

    block = min(times, 32)
    for p in range(parts):
        all_of(first_part + p).wait_recv()
        span = slice(p * PACK, (p + 1) * PACK)
        values = recv[:, span, :].reshape(times * PACK, LANES)
        for t in range(0, times, block):
            these = pl.ds(t, block)
            base = jnp.dot(mix[t * PACK : (t + block) * PACK, :], values, preferred_element_type=jnp.float32)
            base = base.reshape(block, PACK, LANES)
            got = (recv[these, span, :].astype(jnp.float32) - base) * inverse(base + 0.1)
            ratio[these, span, :] = got
            dff[these, span, :] = got.astype(jnp.bfloat16)
        slope[0, span] = (ratio[1, span] - ratio[0, span]).astype(jnp.bfloat16)
        slope[1 : times - 1, span] = ((ratio[2:, span] - ratio[: times - 2, span]) * 0.5).astype(jnp.bfloat16)
        slope[times - 1, span] = (ratio[times - 1, span] - ratio[times - 2, span]).astype(jnp.bfloat16)

    for piece in range(vols + parts):
        all_of(piece).wait_send()

    @pl.when(has_up)
    def _():
        to_up().wait_send()

    @pl.when(has_down)
    def _():
        to_down().wait_send()


def leave(dff, slope, dff_out, slope_out, sem):
    part = dff.shape[0] // 4
    copies = [
        pltpu.make_async_copy(source.at[pl.ds(h * part, part)], target.at[pl.ds(h * part, part)], sem.at[k, h])
        for k, (source, target) in enumerate(((dff, dff_out), (slope, slope_out)))
        for h in range(4)
    ]
    for copy in copies:
        copy.start()
    for copy in copies:
        copy.wait()


def local(n, strips, frames, kappa):
    vols, planes, rows, nx = frames.shape
    times = vols * n
    each = rows // n
    assert planes == 1 and each * 2 == TILE and nx % (2 * LANES) == 0
    depth = each * nx // LANES
    pieces = vols + depth // PACK
    out = jax.ShapeDtypeStruct((times, depth, LANES), jnp.bfloat16)
    f32, bf16 = jnp.float32, jnp.bfloat16
    results = pl.pallas_call(
        functools.partial(kernel, n, strips),
        out_shape=(out, out),
        in_specs=[pl.BlockSpec(memory_space=pltpu.HBM)] * 2,
        out_specs=(pl.BlockSpec(memory_space=pltpu.VMEM),) * 2,
        scratch_shapes=[
            pltpu.VMEM((vols, rows, nx), bf16),
            pltpu.SMEM((vols,), f32),
            pltpu.VMEM((2, vols * TILE, nx), bf16),
            pltpu.VMEM((2, vols * TILE, nx), bf16),
            pltpu.VMEM((vols, TILE, nx), f32),
            pltpu.VMEM((vols, rows + 2 * TILE, nx), f32),
            pltpu.VMEM((2, rows // 2 + 3 * TILE, nx), f32),
            pltpu.VMEM((vols, n, depth, LANES), bf16),
            pltpu.VMEM((times, depth, LANES), bf16),
            pltpu.VMEM((times * PACK, times * PACK), bf16),
            pltpu.VMEM((times, depth, LANES), f32),
            pltpu.SemaphoreType.DMA((vols + 1,)),
            pltpu.SemaphoreType.DMA((2,)),
            pltpu.SemaphoreType.DMA((2,)),
            pltpu.SemaphoreType.DMA((pieces,)),
            pltpu.SemaphoreType.DMA((pieces,)),
            pltpu.SemaphoreType.DMA((vols,)),
        ],
        compiler_params=pltpu.CompilerParams(
            collective_id=0, has_side_effects=True, vmem_limit_bytes=40 * 1024 * 1024),
        cost_estimate=pl.CostEstimate(flops=200_000_000, bytes_accessed=1_000_000, transcendentals=1_000_000),
    )(pltpu.with_memory_space_constraint(frames, pltpu.HBM), pltpu.with_memory_space_constraint(kappa, pltpu.HBM))

    results = pl.pallas_call(
        leave,
        out_shape=(out, out),
        in_specs=[pl.BlockSpec(memory_space=pl.ANY)] * 2,
        out_specs=(pl.BlockSpec(memory_space=pltpu.HBM),) * 2,
        scratch_shapes=[pltpu.SemaphoreType.DMA((2, 4))],
        compiler_params=pltpu.CompilerParams(vmem_limit_bytes=2 * 1024 * 1024),
        cost_estimate=pl.CostEstimate(flops=0, bytes_accessed=1_000_000, transcendentals=0),
    )(*[pltpu.with_memory_space_constraint(x, pltpu.VMEM) for x in results])

    def laid(value):
        value = value.reshape(times, nx // LANES, each, LANES).transpose(0, 2, 1, 3)
        return value.reshape(times, 1, each, 1, nx)

    return laid(results[0]), laid(results[1])


def solution(mesh):
    placed = P(None, None, "vol", "strip", None)
    return jax.shard_map(
        functools.partial(local, mesh.shape["vol"], mesh.shape["strip"]),
        mesh=mesh,
        in_specs=(P("vol", None, "strip", None), P("vol")),
        out_specs=(placed, placed),
        check_vma=False,
    )
```

```python
import functools

import jax
import jax.numpy as jnp
from jax import lax
from jax.experimental import pallas as pl
from jax.experimental.pallas import tpu as pltpu
from jax.sharding import PartitionSpec as P

PASSES = 3
BAND = 16
LANES = 128
TILE = 8
PACK = 16
MESH = pl.DeviceIdType.MESH


def inverse(value):
    guess = pltpu.reciprocal(value, approx=True)
    return guess * (2.0 - value * guess)


def flux(diff):
    return diff * inverse(1.0 + diff * diff)


def shifted_rows(center, below):
    row = lax.broadcasted_iota(jnp.int32, center.shape, 0)
    return pltpu.roll(jnp.where(row == 0, below, center), TILE - 1, 0)


def flux_x(center):
    nx = center.shape[1]
    lane = lax.broadcasted_iota(jnp.int32, (TILE, LANES), 1)
    left = pltpu.roll(center, 1, 1)
    left = jnp.concatenate([jnp.where(lane == 0, 0.0, left[:, :LANES]), left[:, LANES:]], axis=1)
    into = flux(left - center)
    out = pltpu.roll(into, nx - 1, 1)
    edge = flux(center[:, nx - LANES :])
    out = jnp.concatenate([out[:, : nx - LANES], jnp.where(lane == LANES - 1, edge, out[:, nx - LANES :])], axis=1)
    return into - out


def advance(above, tiles, below, emit):
    center = tiles[0]()
    row = lax.broadcasted_iota(jnp.int32, center.shape, 0)
    before = above()
    before = flux(shifted_rows(before, center) - before)
    for i in range(len(tiles)):
        after = tiles[i + 1]() if i + 1 < len(tiles) else below()
        down = flux(shifted_rows(center, after) - center)
        up = pltpu.roll(jnp.where(row == TILE - 1, before, down), 1, 0)
        total = (down - up) + flux_x(center)
        emit(i, center + 0.2 * total)
        before, center = down, after


def folded(value, lower):
    small = lax.broadcasted_iota(jnp.int32, (TILE, LANES), 0) < TILE // 2
    swapped = pltpu.roll(value, TILE // 2, 0)
    first, second = (swapped, value) if lower else (value, swapped)
    parts = []
    for c in range(0, value.shape[1], 2 * LANES):
        parts.append(jnp.where(small, first[:, c : c + LANES], second[:, c + LANES : c + 2 * LANES]))
    return jnp.concatenate(parts, axis=0).astype(jnp.bfloat16)


def kernel(n, strips, frames, kappa, dff, slope, held, kap, rim, halo, beyond, start, field, send, recv, mix, ratio,
           load_sem, halo_send, halo_recv, send_sem, recv_sem, own_sem):
    vols, _, rows, nx = frames.shape
    times, depth, _ = recv.shape
    tiles = rows // TILE
    me = lax.axis_index("vol")
    strip = lax.axis_index("strip")
    has_up = strip > 0
    has_down = strip < strips - 1

    loads = [pltpu.make_async_copy(frames.at[v, 0], held.at[v], load_sem.at[v]) for v in range(vols)]
    load_kappa = pltpu.make_async_copy(kappa, kap, load_sem.at[vols])
    load_kappa.start()
    for load in loads:
        load.start()

    barrier = pltpu.get_barrier_semaphore()

    @pl.loop(1, n)
    def _(k):
        pl.semaphore_signal(barrier, inc=1, device_id={"vol": lax.rem(me + k, n)}, device_id_type=MESH)

    @pl.when(has_up)
    def _():
        pl.semaphore_signal(barrier, inc=1, device_id={"strip": strip - 1}, device_id_type=MESH)

    @pl.when(has_down)
    def _():
        pl.semaphore_signal(barrier, inc=1, device_id={"strip": strip + 1}, device_id_type=MESH)

    def to_up():
        return pltpu.make_async_remote_copy(
            src_ref=rim.at[1], dst_ref=halo.at[1], send_sem=halo_send.at[1], recv_sem=halo_recv.at[1],
            device_id={"strip": strip - 1}, device_id_type=MESH)

    def to_down():
        return pltpu.make_async_remote_copy(
            src_ref=rim.at[0], dst_ref=halo.at[0], send_sem=halo_send.at[0], recv_sem=halo_recv.at[0],
            device_id={"strip": strip + 1}, device_id_type=MESH)

    parts = depth // PACK
    group = n // 2
    side = me // group
    near, first_part = vols - 1, vols

    def sending(v, start, length, piece, to):
        return pltpu.make_async_remote_copy(
            src_ref=send.at[v, to, pl.ds(start, length)], dst_ref=recv.at[me * vols + v, pl.ds(start, length)],
            send_sem=send_sem.at[piece], recv_sem=recv_sem.at[piece],
            device_id={"vol": to}, device_id_type=MESH)

    def joined(to):
        return pltpu.make_async_remote_copy(
            src_ref=send.at[:, to], dst_ref=recv.at[pl.ds(me * vols, vols)],
            send_sem=send_sem.at[near], recv_sem=recv_sem.at[near],
            device_id={"vol": to}, device_id_type=MESH)

    def all_of(piece):
        last = not isinstance(piece, int) or piece >= first_part
        count = (group - 1) * vols if not last and piece == near else group
        these = recv.at[pl.ds(0, count), pl.ds(0, PACK if last else depth)]
        return pltpu.make_async_remote_copy(
            src_ref=these, dst_ref=these, send_sem=send_sem.at[piece], recv_sem=recv_sem.at[piece],
            device_id={"vol": lax.rem(me + 1, n)}, device_id_type=MESH)

    def scaled(block, v):
        return block.astype(jnp.float32) * (1.0 / jnp.full(block.shape, kap[v], jnp.float32))

    def tile(ref, i):
        return ref[pl.ds(pl.multiple_of(i * TILE, TILE), TILE), :]

    def getters(ref, start, count):
        return [functools.partial(tile, ref, start + i) for i in range(count)]

    def ready(to):
        return jnp.logical_not(jnp.logical_or(
            jnp.logical_or(jnp.logical_and(has_up, to == 0), jnp.logical_and(has_down, to == n - 1)), to == me))

    zero = jnp.zeros((TILE, nx), jnp.float32)
    some = tiles // 2
    for buffer in (0, 1):
        field[buffer, :TILE, :] = zero
        field[buffer, (some + 2) * TILE :, :] = zero
    for v in range(vols):
        start[v, :TILE, :] = zero
        start[v, (tiles + 1) * TILE :, :] = zero

    column = lax.broadcasted_iota(jnp.int32, (PACK, times * PACK), 1)
    diagonal = column % PACK == lax.broadcasted_iota(jnp.int32, (PACK, times * PACK), 0)
    source = jnp.where(diagonal, column // PACK, -2 * times - BAND).astype(jnp.float32)

    def weigh(t, _):
        ahead = jnp.maximum(BAND - t, 0)
        behind = jnp.maximum(t + BAND + 1 - times, 0)
        total = (BAND + 1) ** 2 - (ahead * (ahead + 1) + behind * (behind + 1)) // 2
        share = 1.0 / jnp.full((TILE, LANES), total, jnp.int32).astype(jnp.float32)
        raw = jnp.maximum(BAND + 1 - jnp.abs(source - t.astype(jnp.float32)), 0.0)
        raw = raw.reshape(PACK // TILE, TILE, times * PACK)
        weight = jnp.concatenate(
            [raw[:, :, c : c + LANES] * share[None] for c in range(0, times * PACK, LANES)], axis=2)
        mix[pl.ds(pl.multiple_of(t * PACK, PACK), PACK), :] = weight.reshape(PACK, times * PACK).astype(jnp.bfloat16)
        return 0

    lax.fori_loop(0, times, weigh, 0, unroll=4)

    f32 = jnp.float32

    def enter(v):
        loads[v].wait()
        for i in range(rows // PACK):
            start[v, TILE + i * PACK : TILE + (i + 1) * PACK, :] = scaled(held[v, i * PACK : (i + 1) * PACK, :], v)

    load_kappa.wait()
    enter(0)

    @pl.loop(0, 2 * vols)
    def _(unit):
        v = lax.rem(unit, vols)
        away = unit < vols
        half = jnp.where(away, 1 - side, side)
        unscale = jnp.full((TILE, nx), kap[v], jnp.float32)

        base = pl.multiple_of((half * (some - 1) + 1) * TILE, TILE)
        span = (some + 1) * TILE
        field[0, TILE : TILE + span, :] = start[v, pl.ds(base, span), :]

        @pl.loop(0, PASSES)
        def _(step):
            old, new = field.at[step % 2], field.at[(step + 1) % 2]

            def keep(i, value):
                new[(i + 1) * TILE : (i + 2) * TILE, :] = value

            get = getters(old, 0, some + 3)
            advance(get[0], get[1:-1], get[-1], keep)

        @pl.loop(0, some)
        def _(i):
            value = tile(field.at[PASSES % 2], half + 1 + i) * unscale
            to = half * group + 2 * i
            send[v, to] = folded(value, False)
            send[v, to + 1] = folded(value, True)

        @pl.when(unit == 0)
        def _():
            for w in range(1, vols):
                enter(w)
            rim[1] = jnp.concatenate(
                [held[w, :PACK, :].astype(f32)[:TILE] for w in range(vols)], axis=0).astype(jnp.bfloat16)
            rim[0] = jnp.concatenate(
                [held[w, rows - PACK :, :].astype(f32)[TILE:] for w in range(vols)], axis=0).astype(jnp.bfloat16)
            pl.semaphore_wait(barrier, n - 1 + has_up.astype(jnp.int32) + has_down.astype(jnp.int32))

            @pl.when(has_up)
            def _():
                to_up().start()

            @pl.when(has_down)
            def _():
                to_down().start()

        def each(copy):
            def step(j, _):
                to = half * group + lax.rem(me + j, group)

                @pl.when(ready(to))
                def _():
                    copy(to).start()

                return 0

            lax.fori_loop(0, group, step, 0, unroll=group <= 8)

        last = v == vols - 1

        @pl.when(jnp.logical_and(away, jnp.logical_not(last)))
        def _():
            each(lambda to: sending(v, 0, depth, v, to))

        @pl.when(jnp.logical_and(away, last))
        def _():
            for p in range(parts):
                each(lambda to: sending(v, p * PACK, PACK, first_part + p, to))

        @pl.when(jnp.logical_and(last, jnp.logical_not(away)))
        def _():
            each(joined)

    def edge(own, other, own_first, v):
        def step(_, both):
            made = []
            outside = lambda: jnp.zeros_like(own)
            advance(outside, [lambda x=x: x for x in both], outside, lambda i, value: made.append(value))
            return tuple(made)

        both = lax.fori_loop(0, PASSES, step, (own, other) if own_first else (other, own))
        return both[0 if own_first else 1] * jnp.full(own.shape, kap[v], jnp.float32)

    def edges(to, copy, which, own_first):
        copy.wait_recv()
        got = halo[which].astype(f32)
        for v in range(vols):
            beyond[v] = got[v * TILE : (v + 1) * TILE]

        @pl.loop(0, vols)
        def _(v):
            other = scaled(beyond[v], v)
            at = tiles if own_first else 1
            mine = start[v, at * TILE : (at + 1) * TILE, :]
            send[v, to] = folded(edge(mine, other, own_first, v), own_first)

        same = side == to // group

        @pl.when(jnp.logical_and(same, me != to))
        def _():
            joined(to).start()

        @pl.when(jnp.logical_not(same))
        def _():
            for v in range(vols - 1):
                sending(v, 0, depth, v, to).start()
            for p in range(parts):
                sending(vols - 1, p * PACK, PACK, first_part + p, to).start()

    @pl.when(has_up)
    def _():
        edges(0, to_down(), 0, False)

    @pl.when(has_down)
    def _():
        edges(n - 1, to_up(), 1, True)

    own = [pltpu.make_async_copy(send.at[v, me], recv.at[me * vols + v], own_sem.at[v]) for v in range(vols)]
    for copy in own:
        copy.start()

    for copy in own:
        copy.wait()
    for piece in range(vols):
        all_of(piece).wait_recv()

    block = 8
    ratio[0] = jnp.zeros(ratio.shape[1:], f32)
    ratio[times + 1] = jnp.zeros(ratio.shape[1:], f32)

    @pl.loop(0, parts)
    def _(p):
        all_of(first_part + p).wait_recv()
        span = pl.ds(pl.multiple_of(p * PACK, PACK), PACK)
        values = recv[:, span, :].reshape(times * PACK, LANES)

        @pl.loop(0, times // block)
        def _(b):
            these = pl.ds(b * block, block)
            lines = pl.ds(pl.multiple_of(b * block * PACK, block * PACK), block * PACK)
            base = jnp.dot(mix[lines, :], values, preferred_element_type=jnp.float32)
            base = base.reshape(block, PACK, LANES)
            got = (recv[these, span, :].astype(jnp.float32) - base) * inverse(base + 0.1)
            ratio[pl.ds(b * block + 1, block), span, :] = got
            dff[these, span, :] = got.astype(jnp.bfloat16)

        @pl.loop(0, times // block)
        def _(b):
            t = b * block
            change = (ratio[pl.ds(t + 2, block), span, :] - ratio[pl.ds(t, block), span, :]) * 0.5
            slope[pl.ds(t, block), span, :] = change.astype(jnp.bfloat16)

        slope[0, span, :] = (ratio[2, span, :] - ratio[1, span, :]).astype(jnp.bfloat16)
        slope[times - 1, span, :] = (ratio[times, span, :] - ratio[times - 1, span, :]).astype(jnp.bfloat16)

    for piece in range(vols + parts):
        all_of(piece).wait_send()

    @pl.when(has_up)
    def _():
        to_up().wait_send()

    @pl.when(has_down)
    def _():
        to_down().wait_send()


def leave(dff, slope, dff_out, slope_out, sem):
    part = dff.shape[0] // 4
    copies = [
        pltpu.make_async_copy(source.at[pl.ds(h * part, part)], target.at[pl.ds(h * part, part)], sem.at[k, h])
        for k, (source, target) in enumerate(((dff, dff_out), (slope, slope_out)))
        for h in range(4)
    ]
    for copy in copies:
        copy.start()
    for copy in copies:
        copy.wait()


def local(n, strips, frames, kappa):
    vols, planes, rows, nx = frames.shape
    times = vols * n
    each = rows // n
    assert planes == 1 and each * 2 == TILE and nx % (2 * LANES) == 0
    depth = each * nx // LANES
    pieces = vols + depth // PACK
    out = jax.ShapeDtypeStruct((times, depth, LANES), jnp.bfloat16)
    f32, bf16 = jnp.float32, jnp.bfloat16
    results = pl.pallas_call(
        functools.partial(kernel, n, strips),
        out_shape=(out, out),
        in_specs=[pl.BlockSpec(memory_space=pltpu.HBM)] * 2,
        out_specs=(pl.BlockSpec(memory_space=pltpu.VMEM),) * 2,
        scratch_shapes=[
            pltpu.VMEM((vols, rows, nx), bf16),
            pltpu.SMEM((vols,), f32),
            pltpu.VMEM((2, vols * TILE, nx), bf16),
            pltpu.VMEM((2, vols * TILE, nx), bf16),
            pltpu.VMEM((vols, TILE, nx), f32),
            pltpu.VMEM((vols, rows + 2 * TILE, nx), f32),
            pltpu.VMEM((2, rows // 2 + 3 * TILE, nx), f32),
            pltpu.VMEM((vols, n, depth, LANES), bf16),
            pltpu.VMEM((times, depth, LANES), bf16),
            pltpu.VMEM((times * PACK, times * PACK), bf16),
            pltpu.VMEM((times + 2, depth, LANES), f32),
            pltpu.SemaphoreType.DMA((vols + 1,)),
            pltpu.SemaphoreType.DMA((2,)),
            pltpu.SemaphoreType.DMA((2,)),
            pltpu.SemaphoreType.DMA((pieces,)),
            pltpu.SemaphoreType.DMA((pieces,)),
            pltpu.SemaphoreType.DMA((vols,)),
        ],
        compiler_params=pltpu.CompilerParams(
            collective_id=0, has_side_effects=True, vmem_limit_bytes=40 * 1024 * 1024),
        cost_estimate=pl.CostEstimate(flops=200_000_000, bytes_accessed=1_000_000, transcendentals=1_000_000),
    )(pltpu.with_memory_space_constraint(frames, pltpu.HBM), pltpu.with_memory_space_constraint(kappa, pltpu.HBM))

    results = pl.pallas_call(
        leave,
        out_shape=(out, out),
        in_specs=[pl.BlockSpec(memory_space=pl.ANY)] * 2,
        out_specs=(pl.BlockSpec(memory_space=pltpu.HBM),) * 2,
        scratch_shapes=[pltpu.SemaphoreType.DMA((2, 4))],
        compiler_params=pltpu.CompilerParams(vmem_limit_bytes=2 * 1024 * 1024),
        cost_estimate=pl.CostEstimate(flops=0, bytes_accessed=1_000_000, transcendentals=0),
    )(*[pltpu.with_memory_space_constraint(x, pltpu.VMEM) for x in results])

    def laid(value):
        value = value.reshape(times, nx // LANES, each, LANES).transpose(0, 2, 1, 3)
        return value.reshape(times, 1, each, 1, nx)

    return laid(results[0]), laid(results[1])


def solution(mesh):
    placed = P(None, None, "vol", "strip", None)
    return jax.shard_map(
        functools.partial(local, mesh.shape["vol"], mesh.shape["strip"]),
        mesh=mesh,
        in_specs=(P("vol", None, "strip", None), P("vol")),
        out_specs=(placed, placed),
        check_vma=False,
    )
```

```python
import functools

import jax
import jax.numpy as jnp
from jax import lax
from jax.experimental import pallas as pl
from jax.experimental.pallas import tpu as pltpu
from jax.sharding import PartitionSpec as P

PASSES = 3
BAND = 16
LANES = 128
TILE = 8
PACK = 16
MESH = pl.DeviceIdType.MESH


def inverse(value):
    guess = pltpu.reciprocal(value, approx=True)
    return guess * (2.0 - value * guess)


def flux(diff):
    return diff * inverse(1.0 + diff * diff)


def shifted_rows(center, below):
    row = lax.broadcasted_iota(jnp.int32, center.shape, 0)
    return pltpu.roll(jnp.where(row == 0, below, center), TILE - 1, 0)


def flux_x(center):
    nx = center.shape[1]
    lane = lax.broadcasted_iota(jnp.int32, (TILE, LANES), 1)
    left = pltpu.roll(center, 1, 1)
    left = jnp.concatenate([jnp.where(lane == 0, 0.0, left[:, :LANES]), left[:, LANES:]], axis=1)
    into = flux(left - center)
    out = pltpu.roll(into, nx - 1, 1)
    edge = flux(center[:, nx - LANES :])
    out = jnp.concatenate([out[:, : nx - LANES], jnp.where(lane == LANES - 1, edge, out[:, nx - LANES :])], axis=1)
    return into - out


def advance(above, tiles, below, emit):
    center = tiles[0]()
    row = lax.broadcasted_iota(jnp.int32, center.shape, 0)
    before = above()
    before = flux(shifted_rows(before, center) - before)
    for i in range(len(tiles)):
        after = tiles[i + 1]() if i + 1 < len(tiles) else below()
        down = flux(shifted_rows(center, after) - center)
        up = pltpu.roll(jnp.where(row == TILE - 1, before, down), 1, 0)
        total = (down - up) + flux_x(center)
        emit(i, center + 0.2 * total)
        before, center = down, after


def folded(value, lower):
    small = lax.broadcasted_iota(jnp.int32, (TILE, LANES), 0) < TILE // 2
    swapped = pltpu.roll(value, TILE // 2, 0)
    first, second = (swapped, value) if lower else (value, swapped)
    parts = []
    for c in range(0, value.shape[1], 2 * LANES):
        parts.append(jnp.where(small, first[:, c : c + LANES], second[:, c + LANES : c + 2 * LANES]))
    return jnp.concatenate(parts, axis=0).astype(jnp.bfloat16)


def kernel(n, strips, frames, kappa, dff, slope, held, kap, rim, halo, beyond, start, field, send, recv, mix, ratio,
           load_sem, halo_send, halo_recv, send_sem, recv_sem, own_sem):
    vols, _, rows, nx = frames.shape
    times, depth, _ = recv.shape
    tiles = rows // TILE
    me = lax.axis_index("vol")
    strip = lax.axis_index("strip")
    has_up = strip > 0
    has_down = strip < strips - 1

    loads = [pltpu.make_async_copy(frames.at[v, 0], held.at[v], load_sem.at[v]) for v in range(vols)]
    load_kappa = pltpu.make_async_copy(kappa, kap, load_sem.at[vols])
    load_kappa.start()
    for load in loads:
        load.start()

    barrier = pltpu.get_barrier_semaphore()

    @pl.loop(1, n)
    def _(k):
        pl.semaphore_signal(barrier, inc=1, device_id={"vol": lax.rem(me + k, n)}, device_id_type=MESH)

    @pl.when(has_up)
    def _():
        pl.semaphore_signal(barrier, inc=1, device_id={"strip": strip - 1}, device_id_type=MESH)

    @pl.when(has_down)
    def _():
        pl.semaphore_signal(barrier, inc=1, device_id={"strip": strip + 1}, device_id_type=MESH)

    def to_up():
        return pltpu.make_async_remote_copy(
            src_ref=rim.at[1], dst_ref=halo.at[1], send_sem=halo_send.at[1], recv_sem=halo_recv.at[1],
            device_id={"strip": strip - 1}, device_id_type=MESH)

    def to_down():
        return pltpu.make_async_remote_copy(
            src_ref=rim.at[0], dst_ref=halo.at[0], send_sem=halo_send.at[0], recv_sem=halo_recv.at[0],
            device_id={"strip": strip + 1}, device_id_type=MESH)

    parts = depth // PACK
    group = n // 2
    side = me // group
    near, first_part = vols - 1, vols

    def sending(v, start, length, piece, to):
        return pltpu.make_async_remote_copy(
            src_ref=send.at[v, to, pl.ds(start, length)], dst_ref=recv.at[me * vols + v, pl.ds(start, length)],
            send_sem=send_sem.at[piece], recv_sem=recv_sem.at[piece],
            device_id={"vol": to}, device_id_type=MESH)

    def joined(to):
        return pltpu.make_async_remote_copy(
            src_ref=send.at[:, to], dst_ref=recv.at[pl.ds(me * vols, vols)],
            send_sem=send_sem.at[near], recv_sem=recv_sem.at[near],
            device_id={"vol": to}, device_id_type=MESH)

    def all_of(piece):
        count = (group - 1) * vols if piece == near else group
        these = recv.at[pl.ds(0, count), pl.ds(0, PACK if piece >= first_part else depth)]
        return pltpu.make_async_remote_copy(
            src_ref=these, dst_ref=these, send_sem=send_sem.at[piece], recv_sem=recv_sem.at[piece],
            device_id={"vol": lax.rem(me + 1, n)}, device_id_type=MESH)

    def scaled(block, v):
        return block.astype(jnp.float32) * (1.0 / jnp.full(block.shape, kap[v], jnp.float32))

    def tile(ref, i):
        return ref[pl.ds(pl.multiple_of(i * TILE, TILE), TILE), :]

    def getters(ref, start, count):
        return [functools.partial(tile, ref, start + i) for i in range(count)]

    def ready(to):
        return jnp.logical_not(jnp.logical_or(
            jnp.logical_or(jnp.logical_and(has_up, to == 0), jnp.logical_and(has_down, to == n - 1)), to == me))

    zero = jnp.zeros((TILE, nx), jnp.float32)
    some = tiles // 2
    for buffer in (0, 1):
        field[buffer, :TILE, :] = zero
        field[buffer, (some + 2) * TILE :, :] = zero
    for v in range(vols):
        start[v, :TILE, :] = zero
        start[v, (tiles + 1) * TILE :, :] = zero

    f32 = jnp.float32

    def enter(v):
        loads[v].wait()
        for i in range(rows // PACK):
            start[v, TILE + i * PACK : TILE + (i + 1) * PACK, :] = scaled(held[v, i * PACK : (i + 1) * PACK, :], v)

    load_kappa.wait()
    enter(0)

    @pl.loop(0, 2 * vols)
    def _(unit):
        v = lax.rem(unit, vols)
        away = unit < vols
        half = jnp.where(away, 1 - side, side)
        unscale = jnp.full((TILE, nx), kap[v], jnp.float32)

        def keep(buffer):
            def emit(i, value):
                field[buffer, (i + 1) * TILE : (i + 2) * TILE, :] = value
            return emit

        def pack(i, value):
            value = value * unscale
            to = half * group + 2 * i
            send[v, to] = folded(value, False)
            send[v, to + 1] = folded(value, True)

        base = half * (some - 1)
        source = start.at[v]
        get = getters(source, base, some + 3)
        advance(get[0], get[1:-1], get[-1], keep(0))
        get = getters(field.at[0], 0, some + 3)
        advance(get[0], get[1:-1], get[-1], keep(1))
        get = getters(field.at[1], half, some + 2)
        advance(get[0], get[1:-1], get[-1], pack)

        @pl.when(unit == 0)
        def _():
            pl.semaphore_wait(barrier, n - 1 + has_up.astype(jnp.int32) + has_down.astype(jnp.int32))

        def each(copy):
            def step(j, _):
                to = half * group + lax.rem(me + j, group)

                @pl.when(ready(to))
                def _():
                    copy(to).start()

                return 0

            lax.fori_loop(0, group, step, 0, unroll=group <= 8)

        last = v == vols - 1

        @pl.when(jnp.logical_and(away, jnp.logical_not(last)))
        def _():
            each(lambda to: sending(v, 0, depth, v, to))

        @pl.when(jnp.logical_and(away, last))
        def _():
            for p in range(parts):
                each(lambda to: sending(v, p * PACK, PACK, first_part + p, to))

        @pl.when(jnp.logical_and(last, jnp.logical_not(away)))
        def _():
            each(joined)

        @pl.when(unit == 0)
        def _():
            for w in range(1, vols):
                enter(w)
            rim[1] = jnp.concatenate(
                [held[w, :PACK, :].astype(f32)[:TILE] for w in range(vols)], axis=0).astype(jnp.bfloat16)
            rim[0] = jnp.concatenate(
                [held[w, rows - PACK :, :].astype(f32)[TILE:] for w in range(vols)], axis=0).astype(jnp.bfloat16)
            @pl.when(has_up)
            def _():
                to_up().start()

            @pl.when(has_down)
            def _():
                to_down().start()

    def edge(own, other, own_first, v):
        both = [own, other] if own_first else [other, own]
        for step in range(PASSES):
            made = []
            outside = lambda: jnp.zeros_like(own)
            advance(outside, [lambda x=x: x for x in both], outside, lambda i, value: made.append(value))
            both = made
        return both[0 if own_first else 1] * jnp.full(own.shape, kap[v], jnp.float32)

    def edges(to, copy, which, own_first):
        copy.wait_recv()
        got = halo[which].astype(f32)
        for v in range(vols):
            beyond[v] = got[v * TILE : (v + 1) * TILE]

        @pl.loop(0, vols)
        def _(v):
            other = scaled(beyond[v], v)
            at = tiles if own_first else 1
            mine = start[v, at * TILE : (at + 1) * TILE, :]
            send[v, to] = folded(edge(mine, other, own_first, v), own_first)

        same = side == to // group

        @pl.when(jnp.logical_and(same, me != to))
        def _():
            joined(to).start()

        @pl.when(jnp.logical_not(same))
        def _():
            for v in range(vols - 1):
                sending(v, 0, depth, v, to).start()
            for p in range(parts):
                sending(vols - 1, p * PACK, PACK, first_part + p, to).start()

    @pl.when(has_up)
    def _():
        edges(0, to_down(), 0, False)

    @pl.when(has_down)
    def _():
        edges(n - 1, to_up(), 1, True)

    own = [pltpu.make_async_copy(send.at[v, me], recv.at[me * vols + v], own_sem.at[v]) for v in range(vols)]
    for copy in own:
        copy.start()

    column = lax.broadcasted_iota(jnp.int32, (PACK, times * PACK), 1)
    diagonal = column % PACK == lax.broadcasted_iota(jnp.int32, (PACK, times * PACK), 0)
    source = jnp.where(diagonal, column // PACK, -2 * times - BAND).astype(jnp.float32)

    def weigh(t, _):
        ahead = jnp.maximum(BAND - t, 0)
        behind = jnp.maximum(t + BAND + 1 - times, 0)
        total = (BAND + 1) ** 2 - (ahead * (ahead + 1) + behind * (behind + 1)) // 2
        share = 1.0 / jnp.full((TILE, LANES), total, jnp.int32).astype(jnp.float32)
        raw = jnp.maximum(BAND + 1 - jnp.abs(source - t.astype(jnp.float32)), 0.0)
        raw = raw.reshape(PACK // TILE, TILE, times * PACK)
        weight = jnp.concatenate(
            [raw[:, :, c : c + LANES] * share[None] for c in range(0, times * PACK, LANES)], axis=2)
        mix[pl.ds(pl.multiple_of(t * PACK, PACK), PACK), :] = weight.reshape(PACK, times * PACK).astype(jnp.bfloat16)
        return 0

    lax.fori_loop(0, times, weigh, 0, unroll=8)

    for copy in own:
        copy.wait()
    for piece in range(vols):
        all_of(piece).wait_recv()

    block = min(times, 32)
    for p in range(parts):
        all_of(first_part + p).wait_recv()
        span = slice(p * PACK, (p + 1) * PACK)
        values = recv[:, span, :].reshape(times * PACK, LANES)
        for t in range(0, times, block):
            these = pl.ds(t, block)
            base = jnp.dot(mix[t * PACK : (t + block) * PACK, :], values, preferred_element_type=jnp.float32)
            base = base.reshape(block, PACK, LANES)
            got = (recv[these, span, :].astype(jnp.float32) - base) * inverse(base + 0.1)
            ratio[these, span, :] = got
            dff[these, span, :] = got.astype(jnp.bfloat16)
        slope[0, span] = (ratio[1, span] - ratio[0, span]).astype(jnp.bfloat16)
        slope[1 : times - 1, span] = ((ratio[2:, span] - ratio[: times - 2, span]) * 0.5).astype(jnp.bfloat16)
        slope[times - 1, span] = (ratio[times - 1, span] - ratio[times - 2, span]).astype(jnp.bfloat16)

    for piece in range(vols + parts):
        all_of(piece).wait_send()

    @pl.when(has_up)
    def _():
        to_up().wait_send()

    @pl.when(has_down)
    def _():
        to_down().wait_send()


def leave(dff, slope, dff_out, slope_out, sem):
    part = dff.shape[0] // 2
    copies = [
        pltpu.make_async_copy(source.at[pl.ds(h * part, part)], target.at[pl.ds(h * part, part)], sem.at[k, h])
        for k, (source, target) in enumerate(((dff, dff_out), (slope, slope_out)))
        for h in range(2)
    ]
    for copy in copies:
        copy.start()
    for copy in copies:
        copy.wait()


def local(n, strips, frames, kappa):
    vols, planes, rows, nx = frames.shape
    times = vols * n
    each = rows // n
    assert planes == 1 and each * 2 == TILE and nx % (2 * LANES) == 0
    depth = each * nx // LANES
    pieces = vols + depth // PACK
    out = jax.ShapeDtypeStruct((times, depth, LANES), jnp.bfloat16)
    f32, bf16 = jnp.float32, jnp.bfloat16
    results = pl.pallas_call(
        functools.partial(kernel, n, strips),
        out_shape=(out, out),
        in_specs=[pl.BlockSpec(memory_space=pltpu.HBM)] * 2,
        out_specs=(pl.BlockSpec(memory_space=pltpu.VMEM),) * 2,
        scratch_shapes=[
            pltpu.VMEM((vols, rows, nx), bf16),
            pltpu.SMEM((vols,), f32),
            pltpu.VMEM((2, vols * TILE, nx), bf16),
            pltpu.VMEM((2, vols * TILE, nx), bf16),
            pltpu.VMEM((vols, TILE, nx), f32),
            pltpu.VMEM((vols, rows + 2 * TILE, nx), f32),
            pltpu.VMEM((2, rows // 2 + 3 * TILE, nx), f32),
            pltpu.VMEM((vols, n, depth, LANES), bf16),
            pltpu.VMEM((times, depth, LANES), bf16),
            pltpu.VMEM((times * PACK, times * PACK), bf16),
            pltpu.VMEM((times, depth, LANES), f32),
            pltpu.SemaphoreType.DMA((vols + 1,)),
            pltpu.SemaphoreType.DMA((2,)),
            pltpu.SemaphoreType.DMA((2,)),
            pltpu.SemaphoreType.DMA((pieces,)),
            pltpu.SemaphoreType.DMA((pieces,)),
            pltpu.SemaphoreType.DMA((vols,)),
        ],
        compiler_params=pltpu.CompilerParams(
            collective_id=0, has_side_effects=True, vmem_limit_bytes=40 * 1024 * 1024),
        cost_estimate=pl.CostEstimate(flops=200_000_000, bytes_accessed=1_000_000, transcendentals=1_000_000),
    )(pltpu.with_memory_space_constraint(frames, pltpu.HBM), pltpu.with_memory_space_constraint(kappa, pltpu.HBM))

    results = pl.pallas_call(
        leave,
        out_shape=(out, out),
        in_specs=[pl.BlockSpec(memory_space=pl.ANY)] * 2,
        out_specs=(pl.BlockSpec(memory_space=pltpu.HBM),) * 2,
        scratch_shapes=[pltpu.SemaphoreType.DMA((2, 2))],
        compiler_params=pltpu.CompilerParams(vmem_limit_bytes=2 * 1024 * 1024),
        cost_estimate=pl.CostEstimate(flops=0, bytes_accessed=1_000_000, transcendentals=0),
    )(*[pltpu.with_memory_space_constraint(x, pltpu.VMEM) for x in results])

    def laid(value):
        value = value.reshape(times, nx // LANES, each, LANES).transpose(0, 2, 1, 3)
        return value.reshape(times, 1, each, 1, nx)

    return laid(results[0]), laid(results[1])


def solution(mesh):
    placed = P(None, None, "vol", "strip", None)
    return jax.shard_map(
        functools.partial(local, mesh.shape["vol"], mesh.shape["strip"]),
        mesh=mesh,
        in_specs=(P("vol", None, "strip", None), P("vol")),
        out_specs=(placed, placed),
        check_vma=False,
    )
```

```python
import functools

import jax
import jax.numpy as jnp
from jax import lax
from jax.experimental import pallas as pl
from jax.experimental.pallas import tpu as pltpu
from jax.sharding import PartitionSpec as P

PASSES = 3
BAND = 16
LANES = 128
TILE = 8
PACK = 16
MESH = pl.DeviceIdType.MESH


def inverse(value):
    guess = pltpu.reciprocal(value, approx=True)
    return guess * (2.0 - value * guess)


def flux(diff):
    return diff * inverse(1.0 + diff * diff)


def shifted_rows(center, below):
    row = lax.broadcasted_iota(jnp.int32, center.shape, 0)
    return pltpu.roll(jnp.where(row == 0, below, center), TILE - 1, 0)


def flux_x(center):
    nx = center.shape[1]
    lane = lax.broadcasted_iota(jnp.int32, (TILE, LANES), 1)
    left = pltpu.roll(center, 1, 1)
    left = jnp.concatenate([jnp.where(lane == 0, 0.0, left[:, :LANES]), left[:, LANES:]], axis=1)
    into = flux(left - center)
    out = pltpu.roll(into, nx - 1, 1)
    edge = flux(center[:, nx - LANES :])
    out = jnp.concatenate([out[:, : nx - LANES], jnp.where(lane == LANES - 1, edge, out[:, nx - LANES :])], axis=1)
    return into - out


def advance(above, tiles, below, emit):
    center = tiles[0]()
    row = lax.broadcasted_iota(jnp.int32, center.shape, 0)
    before = above()
    before = flux(shifted_rows(before, center) - before)
    for i in range(len(tiles)):
        after = tiles[i + 1]() if i + 1 < len(tiles) else below()
        down = flux(shifted_rows(center, after) - center)
        up = pltpu.roll(jnp.where(row == TILE - 1, before, down), 1, 0)
        total = (down - up) + flux_x(center)
        emit(i, center + 0.2 * total)
        before, center = down, after


def folded(value, lower):
    small = lax.broadcasted_iota(jnp.int32, (TILE, LANES), 0) < TILE // 2
    swapped = pltpu.roll(value, TILE // 2, 0)
    first, second = (swapped, value) if lower else (value, swapped)
    parts = []
    for c in range(0, value.shape[1], 2 * LANES):
        parts.append(jnp.where(small, first[:, c : c + LANES], second[:, c + LANES : c + 2 * LANES]))
    return jnp.concatenate(parts, axis=0).astype(jnp.bfloat16)


def kernel(n, strips, frames, kappa, dff, slope, held, kap, rim, halo, beyond, start, field, send, recv, mix, ratio,
           load_sem, halo_send, halo_recv, send_sem, recv_sem, own_sem, near_sem):
    vols, _, rows, nx = frames.shape
    times, depth, _ = recv.shape
    tiles = rows // TILE
    me = lax.axis_index("vol")
    strip = lax.axis_index("strip")
    has_up = strip > 0
    has_down = strip < strips - 1

    loads = [pltpu.make_async_copy(frames.at[v, 0], held.at[v], load_sem.at[v]) for v in range(vols)]
    load_kappa = pltpu.make_async_copy(kappa, kap, load_sem.at[vols])
    load_kappa.start()
    for load in loads:
        load.start()

    barrier = pltpu.get_barrier_semaphore()

    group = n // 2
    side = me // group

    @pl.loop(0, group)
    def _(k):
        to = (1 - side) * group + lax.rem(me + k, group)
        pl.semaphore_signal(barrier, inc=1, device_id={"vol": to}, device_id_type=MESH)

    @pl.when(has_up)
    def _():
        pl.semaphore_signal(barrier, inc=1, device_id={"strip": strip - 1}, device_id_type=MESH)

    @pl.when(has_down)
    def _():
        pl.semaphore_signal(barrier, inc=1, device_id={"strip": strip + 1}, device_id_type=MESH)

    def to_up():
        return pltpu.make_async_remote_copy(
            src_ref=rim.at[1], dst_ref=halo.at[1], send_sem=halo_send.at[1], recv_sem=halo_recv.at[1],
            device_id={"strip": strip - 1}, device_id_type=MESH)

    def to_down():
        return pltpu.make_async_remote_copy(
            src_ref=rim.at[0], dst_ref=halo.at[0], send_sem=halo_send.at[0], recv_sem=halo_recv.at[0],
            device_id={"strip": strip + 1}, device_id_type=MESH)

    parts = depth // PACK
    near, first_part = vols - 1, vols

    def sending(v, start, length, piece, to):
        return pltpu.make_async_remote_copy(
            src_ref=send.at[v, to, pl.ds(start, length)], dst_ref=recv.at[me * vols + v, pl.ds(start, length)],
            send_sem=send_sem.at[piece], recv_sem=recv_sem.at[piece],
            device_id={"vol": to}, device_id_type=MESH)

    def joined(to):
        return pltpu.make_async_remote_copy(
            src_ref=send.at[:, to], dst_ref=recv.at[pl.ds(me * vols, vols)],
            send_sem=send_sem.at[near], recv_sem=recv_sem.at[near],
            device_id={"vol": to}, device_id_type=MESH)

    def all_of(piece):
        count = (group - 1) * vols if piece == near else group
        these = recv.at[pl.ds(0, count), pl.ds(0, PACK if piece >= first_part else depth)]
        return pltpu.make_async_remote_copy(
            src_ref=these, dst_ref=these, send_sem=send_sem.at[piece], recv_sem=recv_sem.at[piece],
            device_id={"vol": lax.rem(me + 1, n)}, device_id_type=MESH)

    def scaled(block, v):
        return block.astype(jnp.float32) * (1.0 / jnp.full(block.shape, kap[v], jnp.float32))

    def tile(ref, i):
        return ref[pl.ds(pl.multiple_of(i * TILE, TILE), TILE), :]

    def getters(ref, start, count):
        return [functools.partial(tile, ref, start + i) for i in range(count)]

    def ready(to):
        return jnp.logical_not(jnp.logical_or(
            jnp.logical_or(jnp.logical_and(has_up, to == 0), jnp.logical_and(has_down, to == n - 1)), to == me))

    zero = jnp.zeros((TILE, nx), jnp.float32)
    some = tiles // 2
    for buffer in (0, 1):
        field[buffer, :TILE, :] = zero
        field[buffer, (some + 2) * TILE :, :] = zero
    for v in range(vols):
        start[v, :TILE, :] = zero
        start[v, (tiles + 1) * TILE :, :] = zero

    f32 = jnp.float32

    def enter(v):
        loads[v].wait()
        for i in range(rows // PACK):
            start[v, TILE + i * PACK : TILE + (i + 1) * PACK, :] = scaled(held[v, i * PACK : (i + 1) * PACK, :], v)

    load_kappa.wait()
    enter(0)

    @pl.loop(0, 2 * vols)
    def _(unit):
        v = lax.rem(unit, vols)
        away = unit < vols
        half = jnp.where(away, 1 - side, side)
        unscale = jnp.full((TILE, nx), kap[v], jnp.float32)

        def keep(buffer):
            def emit(i, value):
                field[buffer, (i + 1) * TILE : (i + 2) * TILE, :] = value
            return emit

        def pack(i, value):
            value = value * unscale
            to = half * group + 2 * i
            send[v, to] = folded(value, False)
            send[v, to + 1] = folded(value, True)

        base = half * (some - 1)
        source = start.at[v]
        get = getters(source, base, some + 3)
        advance(get[0], get[1:-1], get[-1], keep(0))
        get = getters(field.at[0], 0, some + 3)
        advance(get[0], get[1:-1], get[-1], keep(1))
        get = getters(field.at[1], half, some + 2)
        advance(get[0], get[1:-1], get[-1], pack)

        @pl.when(unit == 0)
        def _():
            pl.semaphore_wait(barrier, group + has_up.astype(jnp.int32) + has_down.astype(jnp.int32))
            pl.semaphore_signal(near_sem, inc=1, device_id={"vol": lax.rem(me + group, n)}, device_id_type=MESH)

        def each(copy):
            def step(j, _):
                to = half * group + lax.rem(me + j, group)

                @pl.when(ready(to))
                def _():
                    copy(to).start()

                return 0

            lax.fori_loop(0, group, step, 0, unroll=group <= 8)

        last = v == vols - 1

        @pl.when(jnp.logical_and(away, jnp.logical_not(last)))
        def _():
            each(lambda to: sending(v, 0, depth, v, to))

        @pl.when(jnp.logical_and(away, last))
        def _():
            for p in range(parts):
                each(lambda to: sending(v, p * PACK, PACK, first_part + p, to))

        @pl.when(jnp.logical_and(last, jnp.logical_not(away)))
        def _():
            pl.semaphore_wait(near_sem, 1)
            each(joined)

        @pl.when(unit == 0)
        def _():
            for w in range(1, vols):
                enter(w)
            rim[1] = jnp.concatenate(
                [held[w, :PACK, :].astype(f32)[:TILE] for w in range(vols)], axis=0).astype(jnp.bfloat16)
            rim[0] = jnp.concatenate(
                [held[w, rows - PACK :, :].astype(f32)[TILE:] for w in range(vols)], axis=0).astype(jnp.bfloat16)
            @pl.when(has_up)
            def _():
                to_up().start()

            @pl.when(has_down)
            def _():
                to_down().start()

    def edge(own, other, own_first, v):
        both = [own, other] if own_first else [other, own]
        for step in range(PASSES):
            made = []
            outside = lambda: jnp.zeros_like(own)
            advance(outside, [lambda x=x: x for x in both], outside, lambda i, value: made.append(value))
            both = made
        return both[0 if own_first else 1] * jnp.full(own.shape, kap[v], jnp.float32)

    def edges(to, copy, which, own_first):
        copy.wait_recv()
        got = halo[which].astype(f32)
        for v in range(vols):
            beyond[v] = got[v * TILE : (v + 1) * TILE]

        @pl.loop(0, vols)
        def _(v):
            other = scaled(beyond[v], v)
            at = tiles if own_first else 1
            mine = start[v, at * TILE : (at + 1) * TILE, :]
            send[v, to] = folded(edge(mine, other, own_first, v), own_first)

        same = side == to // group

        @pl.when(jnp.logical_and(same, me != to))
        def _():
            joined(to).start()

        @pl.when(jnp.logical_not(same))
        def _():
            for v in range(vols - 1):
                sending(v, 0, depth, v, to).start()
            for p in range(parts):
                sending(vols - 1, p * PACK, PACK, first_part + p, to).start()

    @pl.when(has_up)
    def _():
        edges(0, to_down(), 0, False)

    @pl.when(has_down)
    def _():
        edges(n - 1, to_up(), 1, True)

    own = [pltpu.make_async_copy(send.at[v, me], recv.at[me * vols + v], own_sem.at[v]) for v in range(vols)]
    for copy in own:
        copy.start()

    column = lax.broadcasted_iota(jnp.int32, (PACK, times * PACK), 1)
    diagonal = column % PACK == lax.broadcasted_iota(jnp.int32, (PACK, times * PACK), 0)
    source = jnp.where(diagonal, column // PACK, -2 * times - BAND).astype(jnp.float32)

    def weigh(t, _):
        ahead = jnp.maximum(BAND - t, 0)
        behind = jnp.maximum(t + BAND + 1 - times, 0)
        total = (BAND + 1) ** 2 - (ahead * (ahead + 1) + behind * (behind + 1)) // 2
        share = 1.0 / jnp.full((TILE, LANES), total, jnp.int32).astype(jnp.float32)
        raw = jnp.maximum(BAND + 1 - jnp.abs(source - t.astype(jnp.float32)), 0.0)
        raw = raw.reshape(PACK // TILE, TILE, times * PACK)
        weight = jnp.concatenate(
            [raw[:, :, c : c + LANES] * share[None] for c in range(0, times * PACK, LANES)], axis=2)
        mix[pl.ds(pl.multiple_of(t * PACK, PACK), PACK), :] = weight.reshape(PACK, times * PACK).astype(jnp.bfloat16)
        return 0

    lax.fori_loop(0, times, weigh, 0, unroll=8)

    for copy in own:
        copy.wait()
    for piece in range(vols):
        all_of(piece).wait_recv()

    block = min(times, 32)
    for p in range(parts):
        all_of(first_part + p).wait_recv()
        span = slice(p * PACK, (p + 1) * PACK)
        values = recv[:, span, :].reshape(times * PACK, LANES)
        for t in range(0, times, block):
            these = pl.ds(t, block)
            base = jnp.dot(mix[t * PACK : (t + block) * PACK, :], values, preferred_element_type=jnp.float32)
            base = base.reshape(block, PACK, LANES)
            got = (recv[these, span, :].astype(jnp.float32) - base) * inverse(base + 0.1)
            ratio[these, span, :] = got
            dff[these, span, :] = got.astype(jnp.bfloat16)
        slope[0, span] = (ratio[1, span] - ratio[0, span]).astype(jnp.bfloat16)
        slope[1 : times - 1, span] = ((ratio[2:, span] - ratio[: times - 2, span]) * 0.5).astype(jnp.bfloat16)
        slope[times - 1, span] = (ratio[times - 1, span] - ratio[times - 2, span]).astype(jnp.bfloat16)

    for piece in range(vols + parts):
        all_of(piece).wait_send()

    @pl.when(has_up)
    def _():
        to_up().wait_send()

    @pl.when(has_down)
    def _():
        to_down().wait_send()


def leave(dff, slope, dff_out, slope_out, sem):
    part = dff.shape[0] // 2
    copies = [
        pltpu.make_async_copy(source.at[pl.ds(h * part, part)], target.at[pl.ds(h * part, part)], sem.at[k, h])
        for k, (source, target) in enumerate(((dff, dff_out), (slope, slope_out)))
        for h in range(2)
    ]
    for copy in copies:
        copy.start()
    for copy in copies:
        copy.wait()


def local(n, strips, frames, kappa):
    vols, planes, rows, nx = frames.shape
    times = vols * n
    each = rows // n
    assert planes == 1 and each * 2 == TILE and nx % (2 * LANES) == 0
    depth = each * nx // LANES
    pieces = vols + depth // PACK
    out = jax.ShapeDtypeStruct((times, depth, LANES), jnp.bfloat16)
    f32, bf16 = jnp.float32, jnp.bfloat16
    results = pl.pallas_call(
        functools.partial(kernel, n, strips),
        out_shape=(out, out),
        in_specs=[pl.BlockSpec(memory_space=pltpu.HBM)] * 2,
        out_specs=(pl.BlockSpec(memory_space=pltpu.VMEM),) * 2,
        scratch_shapes=[
            pltpu.VMEM((vols, rows, nx), bf16),
            pltpu.SMEM((vols,), f32),
            pltpu.VMEM((2, vols * TILE, nx), bf16),
            pltpu.VMEM((2, vols * TILE, nx), bf16),
            pltpu.VMEM((vols, TILE, nx), f32),
            pltpu.VMEM((vols, rows + 2 * TILE, nx), f32),
            pltpu.VMEM((2, rows // 2 + 3 * TILE, nx), f32),
            pltpu.VMEM((vols, n, depth, LANES), bf16),
            pltpu.VMEM((times, depth, LANES), bf16),
            pltpu.VMEM((times * PACK, times * PACK), bf16),
            pltpu.VMEM((times, depth, LANES), f32),
            pltpu.SemaphoreType.DMA((vols + 1,)),
            pltpu.SemaphoreType.DMA((2,)),
            pltpu.SemaphoreType.DMA((2,)),
            pltpu.SemaphoreType.DMA((pieces,)),
            pltpu.SemaphoreType.DMA((pieces,)),
            pltpu.SemaphoreType.DMA((vols,)),
            pltpu.SemaphoreType.REGULAR,
        ],
        compiler_params=pltpu.CompilerParams(
            collective_id=0, has_side_effects=True, vmem_limit_bytes=40 * 1024 * 1024),
        cost_estimate=pl.CostEstimate(flops=200_000_000, bytes_accessed=1_000_000, transcendentals=1_000_000),
    )(pltpu.with_memory_space_constraint(frames, pltpu.HBM), pltpu.with_memory_space_constraint(kappa, pltpu.HBM))

    results = pl.pallas_call(
        leave,
        out_shape=(out, out),
        in_specs=[pl.BlockSpec(memory_space=pl.ANY)] * 2,
        out_specs=(pl.BlockSpec(memory_space=pltpu.HBM),) * 2,
        scratch_shapes=[pltpu.SemaphoreType.DMA((2, 2))],
        compiler_params=pltpu.CompilerParams(vmem_limit_bytes=2 * 1024 * 1024),
        cost_estimate=pl.CostEstimate(flops=0, bytes_accessed=1_000_000, transcendentals=0),
    )(*[pltpu.with_memory_space_constraint(x, pltpu.VMEM) for x in results])

    def laid(value):
        value = value.reshape(times, nx // LANES, each, LANES).transpose(0, 2, 1, 3)
        return value.reshape(times, 1, each, 1, nx)

    return laid(results[0]), laid(results[1])


def solution(mesh):
    placed = P(None, None, "vol", "strip", None)
    return jax.shard_map(
        functools.partial(local, mesh.shape["vol"], mesh.shape["strip"]),
        mesh=mesh,
        in_specs=(P("vol", None, "strip", None), P("vol")),
        out_specs=(placed, placed),
        check_vma=False,
    )
```
